32 devices in a mesh: groups: 2 (over x), rows: 16 (over z, y, core).
Axes of the slice: x: 2, y: 2, z: 4, core: 2. Of those that a mesh axis runs over, the one named last changes fastest.
Arguments:
- pixels: bfloat16 [128, 16, 512], P(('groups', 'rows')), parts along dimension 0, may hold values from -6 to 6
- weight_first: bfloat16 [3, 3, 512, 512], replicated, may hold values from -0.09375 to 0.09375
- weight_second: bfloat16 [3, 3, 512, 512], replicated, may hold values from -0.09375 to 0.09375
- weight_mix: bfloat16 [3, 3, 2048, 2048], P(None, None, None, 'rows'), may hold values from -0.046875 to 0.046875
- weight_out: bfloat16 [3, 3, 2048, 2048], P(None, None, 'rows'), may hold values from -0.046875 to 0.046875
Outputs:
- latent_out: bfloat16 [32, 4, 2048], P(('groups', 'rows')), parts along dimension 0
The draws below stay inside these ranges and needn't reach their ends.
There are 2 independent parts, one for each index of `groups`. The reference program is written for one: setup_inputs(seed, part) draws one part's arguments, and reference() takes and returns one part's arrays. A program takes and returns all parts, laid end to end along the dimension named above; an argument that names none is the same for every part. Nothing has to cross between parts.
All inputs are finite; a program needn't handle non-finite values.
Results may differ from the reference program's by a relative error of at most 0.014.
Values may be sent and summed in bfloat16 or wider, within the bound.
A program may use at most 64 MiB of HBM per device.

```python
import jax
import jax.numpy as jnp

CH = 512
WD = 16
CL = 2048
HT = 64


def block_scale(stream_key, shape, shards, least, top_value):
    level, own = 1.0, jax.random.fold_in(stream_key, 6)
    for dim, parts in shards:
        heights = jnp.exp(jax.random.uniform(jax.random.fold_in(own, dim), (parts,), jnp.float32, least / len(shards), top_value / len(shards)))
        level = level * jnp.repeat(heights, shape[dim] // parts).reshape([-1 if axis == dim else 1 for axis in range(len(shape))])
    return level


def scatter_about(own_key, shape, scale, most, shards=(), kind=jnp.bfloat16):
    entries = scale * jax.random.normal(own_key, shape, jnp.float32)
    if shards:
        entries = entries * block_scale(own_key, shape, shards, -0.22, 0.18)
    return jnp.clip(entries, -most, most).astype(kind)


def setup_inputs(seed: int = 0, part: int = 0) -> dict:
    key_of = jax.random.split(jax.random.key(seed), 6)
    part_keys = jax.random.split(jax.random.fold_in(key_of[5], part), 6)
    pixels = scatter_about(part_keys[0], (HT, WD, CH), 1.0, 6.0, ((0, 16),))
    weight_first = scatter_about(key_of[1], (3, 3, CH, CH), (9 * CH) ** -0.5, 0.09375)
    weight_second = scatter_about(key_of[2], (3, 3, CH, CH), (9 * CH) ** -0.5, 0.09375)
    weight_mix = scatter_about(key_of[3], (3, 3, CL, CL), (9 * CL) ** -0.5, 0.046875, ((3, 16),))
    weight_out = scatter_about(key_of[4], (3, 3, CL, CL), (9 * CL) ** -0.5, 0.046875, ((2, 16),))
    return dict(pixels=pixels, weight_first=weight_first, weight_second=weight_second, weight_mix=weight_mix, weight_out=weight_out)


def conv_same(feature, weight):
    padded = jnp.pad(feature, ((1, 1), (1, 1), (0, 0)))
    row_count = feature.shape[0]
    col_count = feature.shape[1]
    summed = jnp.zeros((row_count, col_count, weight.shape[3]), jnp.float32)
    for row_tap in range(3):
        for col_tap in range(3):
            summed = summed + jnp.dot(padded[row_tap:row_tap + row_count, col_tap:col_tap + col_count], weight[row_tap, col_tap], preferred_element_type=jnp.float32)
    return summed


def unshuffle_average(feature):
    row_count, col_count, chan_count = feature.shape
    widened = feature.astype(jnp.float32).reshape(row_count // 2, 2, col_count // 2, 2, chan_count)
    paired = (widened[:, :, :, 0] + widened[:, :, :, 1]) * 0.5
    return jnp.transpose(paired, (0, 2, 3, 1)).reshape(row_count // 2, col_count // 2, 2 * chan_count).astype(jnp.bfloat16)


def reference(pixels, weight_first, weight_second, weight_mix, weight_out):
    activated = jax.nn.silu(conv_same(pixels, weight_first)).astype(jnp.bfloat16)
    block_out = (pixels.astype(jnp.float32) + conv_same(activated, weight_second)).astype(jnp.bfloat16)
    half_res = unshuffle_average(block_out)
    latent = unshuffle_average(half_res)
    hidden = jax.nn.silu(conv_same(latent, weight_mix)).astype(jnp.bfloat16)
    return (latent.astype(jnp.float32) + conv_same(hidden, weight_out)).astype(jnp.bfloat16)
```

```python
import functools

import jax
import jax.numpy as jnp
from jax import lax
from jax.experimental import pallas as pl
from jax.experimental.pallas import tpu as pltpu
from jax.sharding import PartitionSpec as P

MESH = pl.DeviceIdType.MESH
BF16 = jnp.bfloat16
F32 = jnp.float32


def quotient(value, divisor):
    if divisor & (divisor - 1) == 0:
        return lax.shift_right_logical(value, divisor.bit_length() - 1)
    return value // divisor


def remainder(value, divisor):
    if divisor & (divisor - 1) == 0:
        return value & (divisor - 1)
    return value % divisor


def index(shape, dim):
    return lax.broadcasted_iota(jnp.int32, shape, dim)


def selection(mask, entry):
    return jnp.where(mask, entry, 0.0).astype(BF16)


def dot(left, right):
    return jnp.dot(left, right, preferred_element_type=F32)


def silu(value):
    return value / (1.0 + jnp.exp(-value))


def column_taps(value, cols):
    length = value.shape[0]
    col = remainder(index(value.shape, 0), cols)
    left = jnp.where(col == 0, 0.0, pltpu.roll(value, 1, 0))
    right = jnp.where(col == cols - 1, 0.0, pltpu.roll(value, length - 1, 0))
    return jnp.concatenate([left.astype(BF16), value.astype(BF16), right.astype(BF16)], axis=1)


def latent_tap(value, tap, rows, cols):
    row_step, col_step = tap // 3 - 1, tap % 3 - 1
    step = row_step * cols + col_step
    if step == 0:
        return value
    length = rows * cols
    place = index(value.shape, 0)
    row, col = quotient(place, cols) + row_step, remainder(place, cols) + col_step
    inside = (row >= 0) & (row < rows) & (col >= 0) & (col < cols)
    return jnp.where(inside, pltpu.roll(value, (-step) % length, 0), 0.0)


def kernel(
    n, px, w1, w2, wm, wo, out,
    ext, w1v, w2v, wmv, wov, mix_sel, sort_sel, back_sel, gathered, latents, outgoing, incoming,
    wsem, psem, hsend, hrecv, gsend, grecv, ssend, srecv,
):
    me = lax.axis_index("rows")
    rows, cols, ch = px.shape
    oc = wmv.shape[-1]
    lc = cols // 4
    nk = 16 // lc
    lw = 4 * ch // nk
    cw = ch // nk
    gs = min(n, 16)
    span = gs * lc
    pos = n * lc

    own_pixels = pltpu.make_async_copy(px, ext.at[pl.ds(2, rows)], psem)
    own_pixels.start()
    loads = []
    for which, (src, dst) in enumerate(((w1, w1v), (w2, w2v), (wm, wmv), (wo, wov))):
        loads.append([pltpu.make_async_copy(src.at[a], dst.at[a], wsem.at[which, a]) for a in range(3)])
        for load in loads[-1]:
            load.start()

    barrier = pltpu.get_barrier_semaphore()

    def greet(off, carry):
        pl.semaphore_signal(barrier, inc=1, device_id={"rows": lax.rem(me + off, n)}, device_id_type=MESH)
        return carry

    lax.fori_loop(1, n, greet, 0)

    blank = jnp.zeros((2, cols, ch), BF16)

    @pl.when(me == 0)
    def _():
        ext[pl.ds(0, 2)] = blank

    @pl.when(me == n - 1)
    def _():
        ext[pl.ds(rows + 2, 2)] = blank

    pl.semaphore_wait(barrier, n - 1)

    down = pltpu.make_async_remote_copy(
        src_ref=px.at[pl.ds(rows - 2, 2)], dst_ref=ext.at[pl.ds(0, 2)],
        send_sem=hsend.at[0], recv_sem=hrecv.at[0],
        device_id={"rows": lax.rem(me + 1, n)}, device_id_type=MESH,
    )
    up = pltpu.make_async_remote_copy(
        src_ref=px.at[pl.ds(0, 2)], dst_ref=ext.at[pl.ds(rows + 2, 2)],
        send_sem=hsend.at[1], recv_sem=hrecv.at[1],
        device_id={"rows": lax.rem(me + n - 1, n)}, device_id_type=MESH,
    )

    @pl.when(me < n - 1)
    def _():
        down.start()

    @pl.when(me > 0)
    def _():
        up.start()

    shape = (lw, lw)
    row, col = index(shape, 0), index(shape, 1)
    mix_sel[...] = selection(col == remainder(row, cw) * 4 + quotient(row, cw), 1.0)
    shape = (gs * 16, gs * 16)
    row, col = index(shape, 0), index(shape, 1)
    wanted = remainder(quotient(row, lc), gs) * 16 + quotient(row, span) * lc + remainder(row, lc)
    sort_sel[...] = selection(col == wanted, 1.0)
    wanted = remainder(quotient(row, lc), nk) * span + quotient(row, 16) * lc + remainder(row, lc)
    back_sel[...] = selection(col == wanted, 1.0)
    shape = (rows * cols // 2, rows * cols)
    pair_sel = selection(index(shape, 0) == quotient(index(shape, 1), 2), 0.5)
    shape = (64, rows * cols // 2)
    row, col = index(shape, 0), index(shape, 1)
    part = quotient(row, 16)
    strip = 2 * remainder(part, 2) + quotient(part, 2)
    quad_sel = selection(quotient(col, 2) == strip * lc + remainder(row, lc), 0.5)

    own_pixels.wait()

    @pl.when(me > 0)
    def _():
        down.wait_recv()

    @pl.when(me < n - 1)
    def _():
        up.wait_recv()

    pixels = ext[...].reshape((rows + 4) * cols, ch).astype(F32)
    taps = column_taps(pixels, cols)
    summed = jnp.zeros(((rows + 2) * cols, ch), F32)
    for a in range(3):
        loads[0][a].wait()
        summed = summed + dot(taps[a * cols : (a + rows + 2) * cols], w1v[a])
    row = quotient(index(summed.shape, 0), cols)
    outside = ((row == 0) & (me == 0)) | ((row == rows + 1) & (me == n - 1))
    activated = jnp.where(outside, 0.0, silu(summed)).astype(BF16)
    taps = column_taps(activated.astype(F32), cols)
    summed = pixels[2 * cols : (rows + 2) * cols]
    conv = jnp.zeros((rows * cols, ch), F32)
    for a in range(3):
        loads[1][a].wait()
        conv = conv + dot(taps[a * cols : (a + rows) * cols], w2v[a])
    block_out = (summed + conv).astype(BF16)

    half_res = dot(pair_sel, block_out).astype(BF16)
    quads = dot(quad_sel, half_res)
    chunk = quotient(index((16, cw), 0), lc)
    pieces = []
    for q in range(4):
        mine = quads[16 * q : 16 * q + 16]
        piece = mine[:, :cw]
        for k in range(1, nk):
            piece = jnp.where(chunk == k, mine[:, k * cw : (k + 1) * cw], piece)
        pieces.append(piece)
    latent = dot(jnp.concatenate(pieces, axis=1).astype(BF16), mix_sel[...]).astype(BF16)
    gathered[pl.ds(me, 1)] = latent[None]

    def exchange(source, target, send_sem, recv_sem, pick):
        def push(off, carry):
            peer = lax.rem(me + off, n)
            pltpu.make_async_remote_copy(
                src_ref=source.at[peer if pick else me], dst_ref=target.at[me],
                send_sem=send_sem.at[off], recv_sem=recv_sem.at[off],
                device_id={"rows": peer}, device_id_type=MESH,
            ).start()
            return carry

        def take(off, carry):
            peer = lax.rem(me + n - off, n)
            pltpu.make_async_remote_copy(
                src_ref=source.at[peer if pick else me], dst_ref=target.at[peer],
                send_sem=send_sem.at[off], recv_sem=recv_sem.at[off],
                device_id={"rows": peer}, device_id_type=MESH,
            ).wait_recv()
            return carry

        def settle(off, carry):
            peer = lax.rem(me + off, n)
            pltpu.make_async_remote_copy(
                src_ref=source.at[peer if pick else me], dst_ref=target.at[me],
                send_sem=send_sem.at[off], recv_sem=recv_sem.at[off],
                device_id={"rows": peer}, device_id_type=MESH,
            ).wait_send()
            return carry

        lax.fori_loop(1, n, push, 0)
        lax.fori_loop(1, n, take, 0)
        return lambda: lax.fori_loop(1, n, settle, 0)

    settle_latents = exchange(gathered, gathered, gsend, grecv, False)

    for g in range(n // gs):
        block = gathered[pl.ds(g * gs, gs)].reshape(gs * 16, lw)
        ordered = dot(sort_sel[...], block).astype(BF16)
        for k in range(nk):
            latents[pl.ds(g * span, span), pl.ds(k * lw, lw)] = ordered[k * span : (k + 1) * span]

    for load in loads[2]:
        load.wait()
    everywhere = latents[...]
    width = 2 if oc % 128 == 0 else 1
    hidden = jnp.zeros((pos, oc), F32)
    for first in range(0, 9, width):
        group = range(first, min(first + width, 9))
        weights = [wmv[tap // 3, tap % 3] for tap in group]
        weight = weights[0] if len(weights) == 1 else jnp.concatenate(weights, axis=1)
        terms = dot(everywhere, weight)
        for at, tap in enumerate(group):
            hidden = hidden + latent_tap(terms[:, at * oc : (at + 1) * oc], tap, n, lc)
    hidden = silu(hidden).astype(BF16).astype(F32)

    for load in loads[3]:
        load.wait()
    shifted = [latent_tap(hidden, tap, n, lc).astype(BF16) for tap in range(9)]
    parts = []
    if oc % 128 == 0:
        shifted = jnp.concatenate(shifted, axis=1)
        for k in range(nk):
            weight = wov[:, :, pl.ds(k * lw, lw)].reshape(9 * oc, lw)
            parts.append(dot(shifted, weight).astype(BF16))
    else:
        for k in range(nk):
            total = jnp.zeros((pos, lw), F32)
            for tap in range(9):
                total = total + dot(
                    shifted[tap], wov[tap // 3, pl.ds(tap % 3 * oc, oc), pl.ds(k * lw, lw)]
                )
            parts.append(total.astype(BF16))
    for g in range(n // gs):
        block = jnp.concatenate([part[g * span : (g + 1) * span] for part in parts], axis=0)
        outgoing[pl.ds(g * gs, gs)] = dot(back_sel[...], block).astype(BF16).reshape(gs, 16, lw)
    incoming[pl.ds(me, 1)] = outgoing[pl.ds(me, 1)]
    settle_sums = exchange(outgoing, incoming, ssend, srecv, True)
    total = latent.astype(F32) + jnp.sum(incoming[...].astype(F32), axis=0)
    for k in range(nk):
        out[0, :, pl.ds(k * lw, lw)] = total[k * lc : (k + 1) * lc].astype(BF16)

    @pl.when(me < n - 1)
    def _():
        down.wait_send()

    @pl.when(me > 0)
    def _():
        up.wait_send()

    settle_latents()
    settle_sums()


def local(n, pixels, weight_first, weight_second, weight_mix, weight_out):
    rows, cols, ch = pixels.shape
    cl, oc = weight_mix.shape[2:]
    lc = cols // 4
    nk = 16 // lc
    lw = cl // nk
    gs = min(n, 16)
    first = weight_first.reshape(3, 3 * ch, ch)
    second = weight_second.reshape(3, 3 * ch, ch)
    last = weight_out.reshape(3, 3 * oc, cl)
    dma = pltpu.SemaphoreType.DMA
    return pl.pallas_call(
        functools.partial(kernel, n),
        out_shape=jax.ShapeDtypeStruct((rows // 4, lc, cl), BF16),
        in_specs=[pl.BlockSpec(memory_space=pl.ANY)] * 5,
        out_specs=pl.BlockSpec(memory_space=pltpu.VMEM),
        scratch_shapes=[
            pltpu.VMEM((rows + 4, cols, ch), BF16),
            pltpu.VMEM(first.shape, BF16),
            pltpu.VMEM(second.shape, BF16),
            pltpu.VMEM(weight_mix.shape, BF16),
            pltpu.VMEM(last.shape, BF16),
            pltpu.VMEM((lw, lw), BF16),
            pltpu.VMEM((gs * 16, gs * 16), BF16),
            pltpu.VMEM((gs * 16, gs * 16), BF16),
            pltpu.VMEM((n, 16, lw), BF16),
            pltpu.VMEM((n * lc, cl), BF16),
            pltpu.VMEM((n, 16, lw), BF16),
            pltpu.VMEM((n, 16, lw), BF16),
            dma((4, 3)),
            dma,
            dma((2,)),
            dma((2,)),
            dma((n,)),
            dma((n,)),
            dma((n,)),
            dma((n,)),
        ],
        compiler_params=pltpu.CompilerParams(
            collective_id=0, has_side_effects=True, vmem_limit_bytes=56 * 1024 * 1024
        ),
    )(pixels, first, second, weight_mix, last)


def solution(mesh):
    return jax.shard_map(
        functools.partial(local, mesh.shape["rows"]),
        mesh=mesh,
        in_specs=(
            P(("groups", "rows"), None, None),
            P(),
            P(),
            P(None, None, None, "rows"),
            P(None, None, "rows", None),
        ),
        out_specs=P(("groups", "rows"), None, None),
        check_vma=False,
    )
```

```python
import functools

import jax
import jax.numpy as jnp
from jax import lax
from jax.experimental import pallas as pl
from jax.experimental.pallas import tpu as pltpu
from jax.sharding import PartitionSpec as P

MESH = pl.DeviceIdType.MESH
BF16 = jnp.bfloat16
F32 = jnp.float32


def quotient(value, divisor):
    if divisor & (divisor - 1) == 0:
        return lax.shift_right_logical(value, divisor.bit_length() - 1)
    return value // divisor


def remainder(value, divisor):
    if divisor & (divisor - 1) == 0:
        return value & (divisor - 1)
    return value % divisor


def index(shape, dim):
    return lax.broadcasted_iota(jnp.int32, shape, dim)


def selection(mask, entry):
    return jnp.where(mask, entry, 0.0).astype(BF16)


def dot(left, right):
    return jnp.dot(left, right, preferred_element_type=F32)


def silu(value):
    return value / (1.0 + jnp.exp(-value))


def column_taps(value, cols):
    length = value.shape[0]
    col = remainder(index(value.shape, 0), cols)
    left = jnp.where(col == 0, 0.0, pltpu.roll(value, 1, 0))
    right = jnp.where(col == cols - 1, 0.0, pltpu.roll(value, length - 1, 0))
    return jnp.concatenate([left.astype(BF16), value.astype(BF16), right.astype(BF16)], axis=1)


def latent_tap(value, tap, rows, cols):
    row_step, col_step = tap // 3 - 1, tap % 3 - 1
    step = row_step * cols + col_step
    if step == 0:
        return value
    length = rows * cols
    place = index(value.shape, 0)
    row, col = quotient(place, cols) + row_step, remainder(place, cols) + col_step
    inside = (row >= 0) & (row < rows) & (col >= 0) & (col < cols)
    return jnp.where(inside, pltpu.roll(value, (-step) % length, 0), 0.0)


def kernel(
    n, px, w1, w2, wm, wo, out,
    ext, w1v, w2v, wmv, wov, mix_sel, sort_sel, back_sel, gathered, latents, outgoing, swapped, paired, incoming,
    wsem, psem, hsend, hrecv, gsend, grecv, fsend, frecv, xsend, xrecv, ssend, srecv,
):
    me = lax.axis_index("rows")
    core, chip, chips = lax.rem(me, 2), lax.div(me, 2), n // 2
    sibling = me + 1 - 2 * core
    rows, cols, ch = px.shape
    oc = wmv.shape[-1]
    lc = cols // 4
    nk = 16 // lc
    lw = 4 * ch // nk
    cw = ch // nk
    gs = min(n, 16)
    span = gs * lc
    pos = n * lc
    hw = lw // 2

    def twin(off):
        return 2 * lax.rem(chip + off, chips) + core

    own_pixels = pltpu.make_async_copy(px, ext.at[pl.ds(2, rows)], psem)
    own_pixels.start()
    loads = []
    for which, (src, dst) in enumerate(((w1, w1v), (w2, w2v), (wm, wmv), (wo, wov))):
        loads.append([pltpu.make_async_copy(src.at[a], dst.at[a], wsem.at[which, a]) for a in range(3)])
        for load in loads[-1]:
            load.start()

    barrier = pltpu.get_barrier_semaphore()

    def greet(peer):
        pl.semaphore_signal(barrier, inc=1, device_id={"rows": peer}, device_id_type=MESH)

    def greet_chip(off, carry):
        greet(twin(off))
        return carry

    greet(lax.rem(jnp.where(core == 0, me + n - 1, me + 1), n))
    greet(sibling)
    lax.fori_loop(1, chips, greet_chip, 0)

    blank = jnp.zeros((2, cols, ch), BF16)

    @pl.when(me == 0)
    def _():
        ext[pl.ds(0, 2)] = blank

    @pl.when(me == n - 1)
    def _():
        ext[pl.ds(rows + 2, 2)] = blank

    pl.semaphore_wait(barrier, chips + 1)

    down = pltpu.make_async_remote_copy(
        src_ref=px.at[pl.ds(rows - 2, 2)], dst_ref=ext.at[pl.ds(0, 2)],
        send_sem=hsend.at[0], recv_sem=hrecv.at[0],
        device_id={"rows": lax.rem(me + 1, n)}, device_id_type=MESH,
    )
    up = pltpu.make_async_remote_copy(
        src_ref=px.at[pl.ds(0, 2)], dst_ref=ext.at[pl.ds(rows + 2, 2)],
        send_sem=hsend.at[1], recv_sem=hrecv.at[1],
        device_id={"rows": lax.rem(me + n - 1, n)}, device_id_type=MESH,
    )

    @pl.when(me < n - 1)
    def _():
        down.start()

    @pl.when(me > 0)
    def _():
        up.start()

    shape = (lw, lw)
    row, col = index(shape, 0), index(shape, 1)
    mix_sel[...] = selection(col == remainder(row, cw) * 4 + quotient(row, cw), 1.0)
    shape = (gs * 16, gs * 16)
    row, col = index(shape, 0), index(shape, 1)
    wanted = remainder(quotient(row, lc), gs) * 16 + quotient(row, span) * lc + remainder(row, lc)
    sort_sel[...] = selection(col == wanted, 1.0)
    place = quotient(row, 16)
    place = 2 * remainder(place, gs // 2) + quotient(place, gs // 2)
    wanted = remainder(quotient(row, lc), nk) * span + place * lc + remainder(row, lc)
    back_sel[...] = selection(col == wanted, 1.0)
    shape = (rows * cols // 2, rows * cols)
    pair_sel = selection(index(shape, 0) == quotient(index(shape, 1), 2), 0.5)
    shape = (64, rows * cols // 2)
    row, col = index(shape, 0), index(shape, 1)
    part = quotient(row, 16)
    strip = 2 * remainder(part, 2) + quotient(part, 2)
    quad_sel = selection(quotient(col, 2) == strip * lc + remainder(row, lc), 0.5)

    own_pixels.wait()

    @pl.when(me > 0)
    def _():
        down.wait_recv()

    @pl.when(me < n - 1)
    def _():
        up.wait_recv()

    pixels = ext[...].reshape((rows + 4) * cols, ch).astype(F32)
    taps = column_taps(pixels, cols)
    summed = jnp.zeros(((rows + 2) * cols, ch), F32)
    for a in range(3):
        loads[0][a].wait()
        summed = summed + dot(taps[a * cols : (a + rows + 2) * cols], w1v[a])
    row = quotient(index(summed.shape, 0), cols)
    outside = ((row == 0) & (me == 0)) | ((row == rows + 1) & (me == n - 1))
    activated = jnp.where(outside, 0.0, silu(summed)).astype(BF16)
    taps = column_taps(activated.astype(F32), cols)
    summed = pixels[2 * cols : (rows + 2) * cols]
    conv = jnp.zeros((rows * cols, ch), F32)
    for a in range(3):
        loads[1][a].wait()
        conv = conv + dot(taps[a * cols : (a + rows) * cols], w2v[a])
    block_out = (summed + conv).astype(BF16)

    half_res = dot(pair_sel, block_out).astype(BF16)
    quads = dot(quad_sel, half_res)
    chunk = quotient(index((16, cw), 0), lc)
    pieces = []
    for q in range(4):
        mine = quads[16 * q : 16 * q + 16]
        piece = mine[:, :cw]
        for k in range(1, nk):
            piece = jnp.where(chunk == k, mine[:, k * cw : (k + 1) * cw], piece)
        pieces.append(piece)
    latent = dot(jnp.concatenate(pieces, axis=1).astype(BF16), mix_sel[...]).astype(BF16)
    gathered[pl.ds(me, 1)] = latent[None]

    def handover(off):
        slot = gathered.at[twin(off)]
        return pltpu.make_async_remote_copy(
            src_ref=slot, dst_ref=slot, send_sem=fsend.at[off], recv_sem=frecv.at[off],
            device_id={"rows": sibling}, device_id_type=MESH,
        )

    def spread(off, slot):
        return pltpu.make_async_remote_copy(
            src_ref=gathered.at[slot], dst_ref=gathered.at[slot],
            send_sem=gsend.at[off], recv_sem=grecv.at[off],
            device_id={"rows": twin(off)}, device_id_type=MESH,
        )

    def push_latent(off, carry):
        spread(off, me).start()
        return carry

    def pass_on(off, carry):
        spread(off, twin(chips - off)).wait_recv()
        handover(chips - off).start()
        return carry

    def take_latent(off, carry):
        slot = gathered.at[2 * lax.rem(chip + off, chips) + 1 - core]
        pltpu.make_async_remote_copy(
            src_ref=slot, dst_ref=slot, send_sem=fsend.at[off], recv_sem=frecv.at[off],
            device_id={"rows": sibling}, device_id_type=MESH,
        ).wait_recv()
        return carry

    def settle_latent(off, carry):
        spread(off, me).wait_send()
        handover(off).wait_send()
        return carry

    lax.fori_loop(1, chips, push_latent, 0)
    handover(0).start()
    lax.fori_loop(1, chips, pass_on, 0)
    lax.fori_loop(0, chips, take_latent, 0)

    for g in range(n // gs):
        block = gathered[pl.ds(g * gs, gs)].reshape(gs * 16, lw)
        ordered = dot(sort_sel[...], block).astype(BF16)
        for k in range(nk):
            latents[pl.ds(g * span, span), pl.ds(k * lw, lw)] = ordered[k * span : (k + 1) * span]

    for load in loads[2]:
        load.wait()
    everywhere = latents[...]
    width = 2 if oc % 128 == 0 else 1
    hidden = jnp.zeros((pos, oc), F32)
    for first in range(0, 9, width):
        group = range(first, min(first + width, 9))
        weights = [wmv[tap // 3, tap % 3] for tap in group]
        weight = weights[0] if len(weights) == 1 else jnp.concatenate(weights, axis=1)
        terms = dot(everywhere, weight)
        for at, tap in enumerate(group):
            hidden = hidden + latent_tap(terms[:, at * oc : (at + 1) * oc], tap, n, lc)
    hidden = silu(hidden).astype(BF16).astype(F32)

    for load in loads[3]:
        load.wait()
    shifted = [latent_tap(hidden, tap, n, lc).astype(BF16) for tap in range(9)]
    if oc % 128 == 0:
        shifted = jnp.concatenate(shifted, axis=1)

    def contribution(start):
        lanes = pl.ds(start, hw)
        if oc % 128 == 0:
            return dot(shifted, wov[:, :, lanes].reshape(9 * oc, hw)).astype(BF16)
        total = jnp.zeros((pos, hw), F32)
        for tap in range(9):
            total = total + dot(shifted[tap], wov[tap // 3, pl.ds(tap % 3 * oc, oc), lanes])
        return total.astype(BF16)

    def swap(h):
        return pltpu.make_async_remote_copy(
            src_ref=outgoing.at[h, 1 - core], dst_ref=swapped.at[h],
            send_sem=xsend.at[h], recv_sem=xrecv.at[h],
            device_id={"rows": sibling}, device_id_type=MESH,
        )

    def scatter(h, off, slot):
        return pltpu.make_async_remote_copy(
            src_ref=paired.at[h, lax.rem(chip + off, chips)], dst_ref=incoming.at[h, slot],
            send_sem=ssend.at[h, off], recv_sem=srecv.at[h, off],
            device_id={"rows": twin(off)}, device_id_type=MESH,
        )

    def multiply(h):
        parts = [contribution((h * nk + k) * hw) for k in range(nk)]
        for g in range(n // gs):
            block = jnp.concatenate([part[g * span : (g + 1) * span] for part in parts], axis=0)
            block = dot(back_sel[...], block).astype(BF16).reshape(2, gs // 2, 16, hw)
            outgoing[h, :, pl.ds(g * gs // 2, gs // 2)] = block
        swap(h).start()

    def send_sums(h):
        swap(h).wait_recv()
        paired[h] = (outgoing[h, core].astype(F32) + swapped[h].astype(F32)).astype(BF16)

        def push_sum(off, carry):
            scatter(h, off, chip).start()
            return carry

        lax.fori_loop(1, chips, push_sum, 0)
        incoming[h, pl.ds(chip, 1)] = paired[h, pl.ds(chip, 1)]

    multiply(0)
    multiply(1)
    send_sums(0)
    send_sums(1)

    residual = latent.astype(F32)
    for h in range(2):

        def take_sum(off, carry):
            scatter(h, off, lax.rem(chip + chips - off, chips)).wait_recv()
            return carry

        lax.fori_loop(1, chips, take_sum, 0)
        total = jnp.sum(incoming[h].astype(F32), axis=0)
        for k in range(nk):
            whole = h * nk + k
            piece = residual[whole // 2 * lc : (whole // 2 + 1) * lc, whole % 2 * hw : (whole % 2 + 1) * hw]
            out[0, :, pl.ds(whole * hw, hw)] = (total[k * lc : (k + 1) * lc] + piece).astype(BF16)

    @pl.when(me < n - 1)
    def _():
        down.wait_send()

    @pl.when(me > 0)
    def _():
        up.wait_send()

    handover(0).wait_send()
    lax.fori_loop(1, chips, settle_latent, 0)
    for h in range(2):
        swap(h).wait_send()

        def settle_sum(off, carry):
            scatter(h, off, chip).wait_send()
            return carry

        lax.fori_loop(1, chips, settle_sum, 0)


def local(n, pixels, weight_first, weight_second, weight_mix, weight_out):
    rows, cols, ch = pixels.shape
    cl, oc = weight_mix.shape[2:]
    lc = cols // 4
    nk = 16 // lc
    lw = cl // nk
    gs = min(n, 16)
    first = weight_first.reshape(3, 3 * ch, ch)
    second = weight_second.reshape(3, 3 * ch, ch)
    last = weight_out.reshape(3, 3 * oc, cl)
    dma = pltpu.SemaphoreType.DMA
    return pl.pallas_call(
        functools.partial(kernel, n),
        out_shape=jax.ShapeDtypeStruct((rows // 4, lc, cl), BF16),
        in_specs=[pl.BlockSpec(memory_space=pl.ANY)] * 5,
        out_specs=pl.BlockSpec(memory_space=pltpu.VMEM),
        scratch_shapes=[
            pltpu.VMEM((rows + 4, cols, ch), BF16),
            pltpu.VMEM(first.shape, BF16),
            pltpu.VMEM(second.shape, BF16),
            pltpu.VMEM(weight_mix.shape, BF16),
            pltpu.VMEM(last.shape, BF16),
            pltpu.VMEM((lw, lw), BF16),
            pltpu.VMEM((gs * 16, gs * 16), BF16),
            pltpu.VMEM((gs * 16, gs * 16), BF16),
            pltpu.VMEM((n, 16, lw), BF16),
            pltpu.VMEM((n * lc, cl), BF16),
            pltpu.VMEM((2, 2, n // 2, 16, lw // 2), BF16),
            pltpu.VMEM((2, n // 2, 16, lw // 2), BF16),
            pltpu.VMEM((2, n // 2, 16, lw // 2), BF16),
            pltpu.VMEM((2, n // 2, 16, lw // 2), BF16),
            dma((4, 3)),
            dma,
            dma((2,)),
            dma((2,)),
            dma((n // 2,)),
            dma((n // 2,)),
            dma((n // 2,)),
            dma((n // 2,)),
            dma((2,)),
            dma((2,)),
            dma((2, n // 2)),
            dma((2, n // 2)),
        ],
        compiler_params=pltpu.CompilerParams(
            collective_id=0, has_side_effects=True, vmem_limit_bytes=56 * 1024 * 1024
        ),
    )(pixels, first, second, weight_mix, last)


def solution(mesh):
    return jax.shard_map(
        functools.partial(local, mesh.shape["rows"]),
        mesh=mesh,
        in_specs=(
            P(("groups", "rows"), None, None),
            P(),
            P(),
            P(None, None, None, "rows"),
            P(None, None, "rows", None),
        ),
        out_specs=P(("groups", "rows"), None, None),
        check_vma=False,
    )
```

```python
import functools

import jax
import jax.numpy as jnp
from jax import lax
from jax.experimental import pallas as pl
from jax.experimental.pallas import tpu as pltpu
from jax.sharding import PartitionSpec as P

MESH = pl.DeviceIdType.MESH
BF16 = jnp.bfloat16
F32 = jnp.float32


def quotient(value, divisor):
    if divisor & (divisor - 1) == 0:
        return lax.shift_right_logical(value, divisor.bit_length() - 1)
    return value // divisor


def remainder(value, divisor):
    if divisor & (divisor - 1) == 0:
        return value & (divisor - 1)
    return value % divisor


def index(shape, dim):
    return lax.broadcasted_iota(jnp.int32, shape, dim)


def selection(mask, entry):
    return jnp.where(mask, entry, 0.0).astype(BF16)


def dot(left, right):
    return jnp.dot(left, right, preferred_element_type=F32)


def silu(value):
    return value / (1.0 + jnp.exp(-value))


def column_taps(value, cols):
    length = value.shape[0]
    col = remainder(index(value.shape, 0), cols)
    left = jnp.where(col == 0, 0.0, pltpu.roll(value, 1, 0))
    right = jnp.where(col == cols - 1, 0.0, pltpu.roll(value, length - 1, 0))
    return jnp.concatenate([left.astype(BF16), value.astype(BF16), right.astype(BF16)], axis=1)


def latent_tap(value, tap, rows, cols):
    row_step, col_step = tap // 3 - 1, tap % 3 - 1
    step = row_step * cols + col_step
    if step == 0:
        return value
    length = rows * cols
    place = index(value.shape, 0)
    row, col = quotient(place, cols) + row_step, remainder(place, cols) + col_step
    inside = (row >= 0) & (row < rows) & (col >= 0) & (col < cols)
    return jnp.where(inside, pltpu.roll(value, (-step) % length, 0), 0.0)


def kernel(
    n, px, w1, w2, wm, wo, out,
    ext, w1v, w2v, wmv, wov, mix_sel, sort_sel, back_sel, gathered, latents, outgoing, swapped, paired, incoming,
    wsem, psem, hsend, hrecv, gsend, grecv, fsend, frecv, xsend, xrecv, ssend, srecv,
):
    me = lax.axis_index("rows")
    core, chip, chips = lax.rem(me, 2), lax.div(me, 2), n // 2
    sibling = me + 1 - 2 * core
    rows, cols, ch = px.shape
    oc = wmv.shape[-1]
    lc = cols // 4
    nk = 16 // lc
    lw = 4 * ch // nk
    cw = ch // nk
    gs = min(n, 16)
    span = gs * lc
    pos = n * lc
    hw = lw // 2

    def twin(off):
        return 2 * lax.rem(chip + off, chips) + core

    own_pixels = pltpu.make_async_copy(px, ext.at[pl.ds(2, rows)], psem)
    own_pixels.start()
    loads = []
    for which, (src, dst) in enumerate(((w1, w1v), (w2, w2v), (wm, wmv), (wo, wov))):
        loads.append([pltpu.make_async_copy(src.at[a], dst.at[a], wsem.at[which, a]) for a in range(3)])
    for load in loads[0] + loads[1]:
        load.start()

    barrier = pltpu.get_barrier_semaphore()

    def greet(peer):
        pl.semaphore_signal(barrier, inc=1, device_id={"rows": peer}, device_id_type=MESH)

    def greet_chip(off, carry):
        greet(twin(off))
        return carry

    greet(lax.rem(jnp.where(core == 0, me + n - 1, me + 1), n))
    greet(sibling)
    lax.fori_loop(1, chips, greet_chip, 0)

    blank = jnp.zeros((2, cols, ch), BF16)

    @pl.when(me == 0)
    def _():
        ext[pl.ds(0, 2)] = blank

    @pl.when(me == n - 1)
    def _():
        ext[pl.ds(rows + 2, 2)] = blank

    pl.semaphore_wait(barrier, chips + 1)

    down = pltpu.make_async_remote_copy(
        src_ref=px.at[pl.ds(rows - 2, 2)], dst_ref=ext.at[pl.ds(0, 2)],
        send_sem=hsend.at[0], recv_sem=hrecv.at[0],
        device_id={"rows": lax.rem(me + 1, n)}, device_id_type=MESH,
    )
    up = pltpu.make_async_remote_copy(
        src_ref=px.at[pl.ds(0, 2)], dst_ref=ext.at[pl.ds(rows + 2, 2)],
        send_sem=hsend.at[1], recv_sem=hrecv.at[1],
        device_id={"rows": lax.rem(me + n - 1, n)}, device_id_type=MESH,
    )

    @pl.when(me < n - 1)
    def _():
        down.start()

    @pl.when(me > 0)
    def _():
        up.start()

    shape = (lw, lw)
    row, col = index(shape, 0), index(shape, 1)
    mix_sel[...] = selection(col == remainder(row, cw) * 4 + quotient(row, cw), 1.0)
    shape = (gs * 16, gs * 16)
    row, col = index(shape, 0), index(shape, 1)
    wanted = remainder(quotient(row, lc), gs) * 16 + quotient(row, span) * lc + remainder(row, lc)
    sort_sel[...] = selection(col == wanted, 1.0)
    place = quotient(row, 16)
    place = 2 * remainder(place, gs // 2) + quotient(place, gs // 2)
    wanted = remainder(quotient(row, lc), nk) * span + place * lc + remainder(row, lc)
    back_sel[...] = selection(col == wanted, 1.0)
    shape = (rows * cols // 2, rows * cols)
    pair_sel = selection(index(shape, 0) == quotient(index(shape, 1), 2), 0.5)
    shape = (64, rows * cols // 2)
    row, col = index(shape, 0), index(shape, 1)
    part = quotient(row, 16)
    strip = 2 * remainder(part, 2) + quotient(part, 2)
    quad_sel = selection(quotient(col, 2) == strip * lc + remainder(row, lc), 0.5)

    own_pixels.wait()

    @pl.when(me > 0)
    def _():
        down.wait_recv()

    @pl.when(me < n - 1)
    def _():
        up.wait_recv()

    for load in loads[2] + loads[3]:
        load.start()

    pixels = ext[...].reshape((rows + 4) * cols, ch).astype(F32)
    taps = column_taps(pixels, cols)
    summed = jnp.zeros(((rows + 2) * cols, ch), F32)
    for a in range(3):
        loads[0][a].wait()
        summed = summed + dot(taps[a * cols : (a + rows + 2) * cols], w1v[a])
    row = quotient(index(summed.shape, 0), cols)
    outside = ((row == 0) & (me == 0)) | ((row == rows + 1) & (me == n - 1))
    activated = jnp.where(outside, 0.0, silu(summed)).astype(BF16)
    taps = column_taps(activated.astype(F32), cols)
    summed = pixels[2 * cols : (rows + 2) * cols]
    conv = jnp.zeros((rows * cols, ch), F32)
    for a in range(3):
        loads[1][a].wait()
        conv = conv + dot(taps[a * cols : (a + rows) * cols], w2v[a])
    block_out = (summed + conv).astype(BF16)

    half_res = dot(pair_sel, block_out).astype(BF16)
    quads = dot(quad_sel, half_res)
    chunk = quotient(index((16, cw), 0), lc)
    pieces = []
    for q in range(4):
        mine = quads[16 * q : 16 * q + 16]
        piece = mine[:, :cw]
        for k in range(1, nk):
            piece = jnp.where(chunk == k, mine[:, k * cw : (k + 1) * cw], piece)
        pieces.append(piece)
    latent = dot(jnp.concatenate(pieces, axis=1).astype(BF16), mix_sel[...]).astype(BF16)
    gathered[pl.ds(me, 1)] = latent[None]

    def handover(off):
        slot = gathered.at[twin(off)]
        return pltpu.make_async_remote_copy(
            src_ref=slot, dst_ref=slot, send_sem=fsend.at[off], recv_sem=frecv.at[off],
            device_id={"rows": sibling}, device_id_type=MESH,
        )

    def spread(off, slot):
        return pltpu.make_async_remote_copy(
            src_ref=gathered.at[slot], dst_ref=gathered.at[slot],
            send_sem=gsend.at[off], recv_sem=grecv.at[off],
            device_id={"rows": twin(off)}, device_id_type=MESH,
        )

    def push_latent(off, carry):
        spread(off, me).start()
        return carry

    def pass_on(off, carry):
        spread(off, twin(chips - off)).wait_recv()
        handover(chips - off).start()
        return carry

    def take_latent(off, carry):
        slot = gathered.at[2 * lax.rem(chip + off, chips) + 1 - core]
        pltpu.make_async_remote_copy(
            src_ref=slot, dst_ref=slot, send_sem=fsend.at[off], recv_sem=frecv.at[off],
            device_id={"rows": sibling}, device_id_type=MESH,
        ).wait_recv()
        return carry

    def settle_latent(off, carry):
        spread(off, me).wait_send()
        handover(off).wait_send()
        return carry

    lax.fori_loop(1, chips, push_latent, 0)
    handover(0).start()
    lax.fori_loop(1, chips, pass_on, 0)
    lax.fori_loop(0, chips, take_latent, 0)

    for g in range(n // gs):
        block = gathered[pl.ds(g * gs, gs)].reshape(gs * 16, lw)
        ordered = dot(sort_sel[...], block).astype(BF16)
        for k in range(nk):
            latents[pl.ds(g * span, span), pl.ds(k * lw, lw)] = ordered[k * span : (k + 1) * span]

    for load in loads[2]:
        load.wait()
    everywhere = latents[...]
    width = 2 if oc % 128 == 0 else 1
    hidden = jnp.zeros((pos, oc), F32)
    for first in range(0, 9, width):
        group = range(first, min(first + width, 9))
        weights = [wmv[tap // 3, tap % 3] for tap in group]
        weight = weights[0] if len(weights) == 1 else jnp.concatenate(weights, axis=1)
        terms = dot(everywhere, weight)
        for at, tap in enumerate(group):
            hidden = hidden + latent_tap(terms[:, at * oc : (at + 1) * oc], tap, n, lc)
    hidden = silu(hidden).astype(BF16).astype(F32)

    for load in loads[3]:
        load.wait()
    shifted = [latent_tap(hidden, tap, n, lc).astype(BF16) for tap in range(9)]
    if oc % 128 == 0:
        shifted = jnp.concatenate(shifted, axis=1)

    def contribution(start):
        lanes = pl.ds(start, hw)
        if oc % 128 == 0:
            return dot(shifted, wov[:, :, lanes].reshape(9 * oc, hw)).astype(BF16)
        total = jnp.zeros((pos, hw), F32)
        for tap in range(9):
            total = total + dot(shifted[tap], wov[tap // 3, pl.ds(tap % 3 * oc, oc), lanes])
        return total.astype(BF16)

    def swap(h):
        return pltpu.make_async_remote_copy(
            src_ref=outgoing.at[h, 1 - core], dst_ref=swapped.at[h],
            send_sem=xsend.at[h], recv_sem=xrecv.at[h],
            device_id={"rows": sibling}, device_id_type=MESH,
        )

    def scatter(h, off, slot):
        return pltpu.make_async_remote_copy(
            src_ref=paired.at[h, lax.rem(chip + off, chips)], dst_ref=incoming.at[h, slot],
            send_sem=ssend.at[h, off], recv_sem=srecv.at[h, off],
            device_id={"rows": twin(off)}, device_id_type=MESH,
        )

    def multiply(h):
        parts = [contribution((h * nk + k) * hw) for k in range(nk)]
        for g in range(n // gs):
            block = jnp.concatenate([part[g * span : (g + 1) * span] for part in parts], axis=0)
            block = dot(back_sel[...], block).astype(BF16).reshape(2, gs // 2, 16, hw)
            outgoing[h, :, pl.ds(g * gs // 2, gs // 2)] = block
        swap(h).start()

    def send_sums(h):
        swap(h).wait_recv()
        paired[h] = (outgoing[h, core].astype(F32) + swapped[h].astype(F32)).astype(BF16)

        def push_sum(off, carry):
            scatter(h, off, chip).start()
            return carry

        lax.fori_loop(1, chips, push_sum, 0)
        incoming[h, pl.ds(chip, 1)] = paired[h, pl.ds(chip, 1)]

    multiply(0)
    multiply(1)
    send_sums(0)
    send_sums(1)

    @pl.when(me < n - 1)
    def _():
        down.wait_send()

    @pl.when(me > 0)
    def _():
        up.wait_send()

    handover(0).wait_send()
    lax.fori_loop(1, chips, settle_latent, 0)
    residual = latent.astype(F32)
    for h in range(2):

        def take_sum(off, carry):
            scatter(h, off, lax.rem(chip + chips - off, chips)).wait_recv()
            return carry

        lax.fori_loop(1, chips, take_sum, 0)
        total = jnp.sum(incoming[h].astype(F32), axis=0)
        for k in range(nk):
            whole = h * nk + k
            piece = residual[whole // 2 * lc : (whole // 2 + 1) * lc, whole % 2 * hw : (whole % 2 + 1) * hw]
            out[0, :, pl.ds(whole * hw, hw)] = (total[k * lc : (k + 1) * lc] + piece).astype(BF16)

    for h in range(2):
        swap(h).wait_send()

        def settle_sum(off, carry):
            scatter(h, off, chip).wait_send()
            return carry

        lax.fori_loop(1, chips, settle_sum, 0)


def local(n, pixels, weight_first, weight_second, weight_mix, weight_out):
    rows, cols, ch = pixels.shape
    cl, oc = weight_mix.shape[2:]
    lc = cols // 4
    nk = 16 // lc
    lw = cl // nk
    gs = min(n, 16)
    first = weight_first.reshape(3, 3 * ch, ch)
    second = weight_second.reshape(3, 3 * ch, ch)
    last = weight_out.reshape(3, 3 * oc, cl)
    dma = pltpu.SemaphoreType.DMA
    return pl.pallas_call(
        functools.partial(kernel, n),
        out_shape=jax.ShapeDtypeStruct((rows // 4, lc, cl), BF16),
        in_specs=[pl.BlockSpec(memory_space=pl.ANY)] * 5,
        out_specs=pl.BlockSpec(memory_space=pltpu.VMEM),
        scratch_shapes=[
            pltpu.VMEM((rows + 4, cols, ch), BF16),
            pltpu.VMEM(first.shape, BF16),
            pltpu.VMEM(second.shape, BF16),
            pltpu.VMEM(weight_mix.shape, BF16),
            pltpu.VMEM(last.shape, BF16),
            pltpu.VMEM((lw, lw), BF16),
            pltpu.VMEM((gs * 16, gs * 16), BF16),
            pltpu.VMEM((gs * 16, gs * 16), BF16),
            pltpu.VMEM((n, 16, lw), BF16),
            pltpu.VMEM((n * lc, cl), BF16),
            pltpu.VMEM((2, 2, n // 2, 16, lw // 2), BF16),
            pltpu.VMEM((2, n // 2, 16, lw // 2), BF16),
            pltpu.VMEM((2, n // 2, 16, lw // 2), BF16),
            pltpu.VMEM((2, n // 2, 16, lw // 2), BF16),
            dma((4, 3)),
            dma,
            dma((2,)),
            dma((2,)),
            dma((n // 2,)),
            dma((n // 2,)),
            dma((n // 2,)),
            dma((n // 2,)),
            dma((2,)),
            dma((2,)),
            dma((2, n // 2)),
            dma((2, n // 2)),
        ],
        compiler_params=pltpu.CompilerParams(
            collective_id=0, has_side_effects=True, vmem_limit_bytes=56 * 1024 * 1024
        ),
    )(pixels, first, second, weight_mix, last)


def solution(mesh):
    return jax.shard_map(
        functools.partial(local, mesh.shape["rows"]),
        mesh=mesh,
        in_specs=(
            P(("groups", "rows"), None, None),
            P(),
            P(),
            P(None, None, None, "rows"),
            P(None, None, "rows", None),
        ),
        out_specs=P(("groups", "rows"), None, None),
        check_vma=False,
    )
```

```python
import functools

import jax
import jax.numpy as jnp
from jax import lax
from jax.experimental import pallas as pl
from jax.experimental.pallas import tpu as pltpu
from jax.sharding import PartitionSpec as P

MESH = pl.DeviceIdType.MESH
BF16 = jnp.bfloat16
F32 = jnp.float32


def quotient(value, divisor):
    if divisor & (divisor - 1) == 0:
        return lax.shift_right_logical(value, divisor.bit_length() - 1)
    return value // divisor


def remainder(value, divisor):
    if divisor & (divisor - 1) == 0:
        return value & (divisor - 1)
    return value % divisor


def index(shape, dim):
    return lax.broadcasted_iota(jnp.int32, shape, dim)


def selection(mask, entry):
    return jnp.where(mask, entry, 0.0).astype(BF16)


def dot(left, right):
    return jnp.dot(left, right, preferred_element_type=F32)


def silu(value):
    return value / (1.0 + jnp.exp(-value))


def column_taps(value, cols):
    length = value.shape[0]
    col = remainder(index(value.shape, 0), cols)
    left = jnp.where(col == 0, 0.0, pltpu.roll(value, 1, 0))
    right = jnp.where(col == cols - 1, 0.0, pltpu.roll(value, length - 1, 0))
    return jnp.concatenate([left.astype(BF16), value.astype(BF16), right.astype(BF16)], axis=1)


def latent_tap(value, tap, rows, cols):
    row_step, col_step = tap // 3 - 1, tap % 3 - 1
    step = row_step * cols + col_step
    if step == 0:
        return value
    length = rows * cols
    place = index(value.shape, 0)
    row, col = quotient(place, cols) + row_step, remainder(place, cols) + col_step
    inside = (row >= 0) & (row < rows) & (col >= 0) & (col < cols)
    return jnp.where(inside, pltpu.roll(value, (-step) % length, 0), 0.0)


def kernel(
    n, px, w1, w2, wm, wo, out,
    ext, w1v, w2v, wmv, wov, mix_sel, sort_sel, back_sel, gathered, latents, outgoing, swapped, paired, incoming,
    wsem, psem, hsend, hrecv, gsend, grecv, fsend, frecv, xsend, xrecv, ssend, srecv,
):
    me = lax.axis_index("rows")
    core, chip, chips = lax.rem(me, 2), lax.div(me, 2), n // 2
    sibling = me + 1 - 2 * core
    rows, cols, ch = px.shape
    oc = wmv.shape[-1]
    lc = cols // 4
    nk = 16 // lc
    lw = 4 * ch // nk
    cw = ch // (2 * nk)
    gs = min(n, 16)
    span = gs * lc
    pos = n * lc
    hw = lw // 2

    def twin(off):
        return 2 * lax.rem(chip + off, chips) + core

    own_pixels = pltpu.make_async_copy(px, ext.at[pl.ds(2, rows)], psem)
    own_pixels.start()
    loads = []
    for which, (src, dst) in enumerate(((w1, w1v), (w2, w2v), (wm, wmv), (wo, wov))):
        loads.append([pltpu.make_async_copy(src.at[a], dst.at[a], wsem.at[which, a]) for a in range(3)])
    for load in loads[0] + loads[1]:
        load.start()

    barrier = pltpu.get_barrier_semaphore()

    def greet(peer):
        pl.semaphore_signal(barrier, inc=1, device_id={"rows": peer}, device_id_type=MESH)

    def greet_chip(off, carry):
        greet(twin(off))
        return carry

    greet(lax.rem(jnp.where(core == 0, me + n - 1, me + 1), n))
    greet(sibling)
    lax.fori_loop(1, chips, greet_chip, 0)

    blank = jnp.zeros((2, cols, ch), BF16)

    @pl.when(me == 0)
    def _():
        ext[pl.ds(0, 2)] = blank

    @pl.when(me == n - 1)
    def _():
        ext[pl.ds(rows + 2, 2)] = blank

    pl.semaphore_wait(barrier, chips + 1)

    down = pltpu.make_async_remote_copy(
        src_ref=px.at[pl.ds(rows - 2, 2)], dst_ref=ext.at[pl.ds(0, 2)],
        send_sem=hsend.at[0], recv_sem=hrecv.at[0],
        device_id={"rows": lax.rem(me + 1, n)}, device_id_type=MESH,
    )
    up = pltpu.make_async_remote_copy(
        src_ref=px.at[pl.ds(0, 2)], dst_ref=ext.at[pl.ds(rows + 2, 2)],
        send_sem=hsend.at[1], recv_sem=hrecv.at[1],
        device_id={"rows": lax.rem(me + n - 1, n)}, device_id_type=MESH,
    )

    @pl.when(me < n - 1)
    def _():
        down.start()

    @pl.when(me > 0)
    def _():
        up.start()

    shape = (2 * ch, hw)
    row, col = index(shape, 0), index(shape, 1)
    mix_sel[...] = selection(col == remainder(row, cw) * 4 + quotient(row, ch // 2), 1.0)
    shape = (gs * 16, gs * 16)
    row, col = index(shape, 0), index(shape, 1)
    wanted = remainder(quotient(row, lc), gs) * 16 + quotient(row, span) * lc + remainder(row, lc)
    sort_sel[...] = selection(col == wanted, 1.0)
    place = quotient(row, 16)
    place = 2 * remainder(place, gs // 2) + quotient(place, gs // 2)
    wanted = remainder(quotient(row, lc), nk) * span + place * lc + remainder(row, lc)
    back_sel[...] = selection(col == wanted, 1.0)
    shape = (rows * cols // 2, rows * cols)
    pair_sel = selection(index(shape, 0) == quotient(index(shape, 1), 2), 0.5)
    shape = (64, rows * cols // 2)
    row, col = index(shape, 0), index(shape, 1)
    part = quotient(row, 16)
    strip = 2 * remainder(part, 2) + quotient(part, 2)
    quad_sel = selection(quotient(col, 2) == strip * lc + remainder(row, lc), 0.5)

    own_pixels.wait()

    @pl.when(me > 0)
    def _():
        down.wait_recv()

    @pl.when(me < n - 1)
    def _():
        up.wait_recv()

    for load in loads[2] + loads[3]:
        load.start()

    pixels = ext[...].reshape((rows + 4) * cols, ch).astype(F32)
    taps = column_taps(pixels, cols)
    summed = jnp.zeros(((rows + 2) * cols, ch), F32)
    for a in range(3):
        loads[0][a].wait()
        summed = summed + dot(taps[a * cols : (a + rows + 2) * cols], w1v[a])
    row = quotient(index(summed.shape, 0), cols)
    outside = ((row == 0) & (me == 0)) | ((row == rows + 1) & (me == n - 1))
    activated = jnp.where(outside, 0.0, silu(summed)).astype(BF16)
    taps = column_taps(activated.astype(F32), cols)
    own = pixels[2 * cols : (rows + 2) * cols]
    for load in loads[1]:
        load.wait()
    chunk = quotient(index((16, ch // 2), 0), lc) == quotient(index((16, ch // 2), 1), cw)

    def make_latent(h):
        lanes = slice(h * ch // 2, (h + 1) * ch // 2)
        conv = dot(taps[: rows * cols], w2v[0, :, lanes])
        for a in range(1, 3):
            conv = conv + dot(taps[a * cols : (a + rows) * cols], w2v[a, :, lanes])
        block_out = (own[:, lanes] + conv).astype(BF16)
        half_res = dot(pair_sel, block_out).astype(BF16)
        quads = dot(quad_sel, half_res)
        pieces = [jnp.where(chunk, quads[16 * q : 16 * q + 16], 0.0).astype(BF16) for q in range(4)]
        return dot(jnp.concatenate(pieces, axis=1), mix_sel[...]).astype(BF16)

    def handover(h, off):
        slot = gathered.at[h, twin(off)]
        return pltpu.make_async_remote_copy(
            src_ref=slot, dst_ref=slot, send_sem=fsend.at[h, off], recv_sem=frecv.at[h, off],
            device_id={"rows": sibling}, device_id_type=MESH,
        )

    def spread(h, off, slot):
        return pltpu.make_async_remote_copy(
            src_ref=gathered.at[h, slot], dst_ref=gathered.at[h, slot],
            send_sem=gsend.at[h, off], recv_sem=grecv.at[h, off],
            device_id={"rows": twin(off)}, device_id_type=MESH,
        )

    def send_latent(h):
        def push_latent(off, carry):
            spread(h, off, me).start()
            return carry

        lax.fori_loop(1, chips, push_latent, 0)
        handover(h, 0).start()

    def forward_latents(h):
        def pass_on(off, carry):
            spread(h, off, twin(chips - off)).wait_recv()
            handover(h, chips - off).start()
            return carry

        lax.fori_loop(1, chips, pass_on, 0)

    def take_latents(h):
        def take_latent(off, carry):
            slot = gathered.at[h, 2 * lax.rem(chip + off, chips) + 1 - core]
            pltpu.make_async_remote_copy(
                src_ref=slot, dst_ref=slot, send_sem=fsend.at[h, off], recv_sem=frecv.at[h, off],
                device_id={"rows": sibling}, device_id_type=MESH,
            ).wait_recv()
            return carry

        lax.fori_loop(0, chips, take_latent, 0)
        for g in range(n // gs):
            block = gathered[h, pl.ds(g * gs, gs)].reshape(gs * 16, hw)
            ordered = dot(sort_sel[...], block).astype(BF16)
            for k in range(nk):
                latents[h, pl.ds(g * span, span), pl.ds(k * hw, hw)] = ordered[k * span : (k + 1) * span]

    own_latents = []
    for h in range(2):
        own_latents.append(make_latent(h))
        gathered[h, pl.ds(me, 1)] = own_latents[h][None]
        send_latent(h)
    forward_latents(0)
    forward_latents(1)

    for load in loads[2]:
        load.wait()
    width = 2 if oc % 128 == 0 else 1
    groups = [range(first, min(first + width, 9)) for first in range(0, 9, width)]
    terms = [None] * len(groups)
    for h in range(2):
        take_latents(h)
        everywhere = latents[h]
        for at, group in enumerate(groups):
            weights = [wmv[tap // 3, tap % 3, pl.ds(h * nk * hw, nk * hw)] for tap in group]
            weight = weights[0] if len(weights) == 1 else jnp.concatenate(weights, axis=1)
            term = dot(everywhere, weight)
            terms[at] = term if h == 0 else terms[at] + term
    hidden = jnp.zeros((pos, oc), F32)
    for term, group in zip(terms, groups):
        for at, tap in enumerate(group):
            hidden = hidden + latent_tap(term[:, at * oc : (at + 1) * oc], tap, n, lc)
    hidden = silu(hidden).astype(BF16).astype(F32)

    for load in loads[3]:
        load.wait()
    shifted = [latent_tap(hidden, tap, n, lc).astype(BF16) for tap in range(9)]
    if oc % 128 == 0:
        shifted = jnp.concatenate(shifted, axis=1)

    def contribution(start):
        lanes = pl.ds(start, hw)
        if oc % 128 == 0:
            return dot(shifted, wov[:, :, lanes].reshape(9 * oc, hw)).astype(BF16)
        total = jnp.zeros((pos, hw), F32)
        for tap in range(9):
            total = total + dot(shifted[tap], wov[tap // 3, pl.ds(tap % 3 * oc, oc), lanes])
        return total.astype(BF16)

    def swap(h):
        return pltpu.make_async_remote_copy(
            src_ref=outgoing.at[h, 1 - core], dst_ref=swapped.at[h],
            send_sem=xsend.at[h], recv_sem=xrecv.at[h],
            device_id={"rows": sibling}, device_id_type=MESH,
        )

    def scatter(h, off, slot):
        return pltpu.make_async_remote_copy(
            src_ref=paired.at[h, lax.rem(chip + off, chips)], dst_ref=incoming.at[h, slot],
            send_sem=ssend.at[h, off], recv_sem=srecv.at[h, off],
            device_id={"rows": twin(off)}, device_id_type=MESH,
        )

    def multiply(h):
        parts = [contribution((h * nk + k) * hw) for k in range(nk)]
        for g in range(n // gs):
            block = jnp.concatenate([part[g * span : (g + 1) * span] for part in parts], axis=0)
            block = dot(back_sel[...], block).astype(BF16).reshape(2, gs // 2, 16, hw)
            outgoing[h, :, pl.ds(g * gs // 2, gs // 2)] = block
        swap(h).start()

    def send_sums(h):
        swap(h).wait_recv()
        paired[h] = (outgoing[h, core].astype(F32) + swapped[h].astype(F32)).astype(BF16)

        def push_sum(off, carry):
            scatter(h, off, chip).start()
            return carry

        lax.fori_loop(1, chips, push_sum, 0)
        incoming[h, pl.ds(chip, 1)] = paired[h, pl.ds(chip, 1)]

    multiply(0)
    multiply(1)
    send_sums(0)
    send_sums(1)

    @pl.when(me < n - 1)
    def _():
        down.wait_send()

    @pl.when(me > 0)
    def _():
        up.wait_send()

    for h in range(2):

        def settle_latent(off, carry):
            spread(h, off, me).wait_send()
            handover(h, off).wait_send()
            return carry

        handover(h, 0).wait_send()
        lax.fori_loop(1, chips, settle_latent, 0)
    for h in range(2):

        def take_sum(off, carry):
            scatter(h, off, lax.rem(chip + chips - off, chips)).wait_recv()
            return carry

        lax.fori_loop(1, chips, take_sum, 0)
        total = jnp.sum(incoming[h].astype(F32), axis=0) + own_latents[h].astype(F32)
        for k in range(nk):
            out[0, :, pl.ds((h * nk + k) * hw, hw)] = total[k * lc : (k + 1) * lc].astype(BF16)

    for h in range(2):
        swap(h).wait_send()

        def settle_sum(off, carry):
            scatter(h, off, chip).wait_send()
            return carry

        lax.fori_loop(1, chips, settle_sum, 0)


def local(n, pixels, weight_first, weight_second, weight_mix, weight_out):
    rows, cols, ch = pixels.shape
    cl, oc = weight_mix.shape[2:]
    lc = cols // 4
    nk = 16 // lc
    lw = cl // nk
    gs = min(n, 16)
    first = weight_first.reshape(3, 3 * ch, ch)
    second = weight_second.reshape(3, 3 * ch, ch)
    last = weight_out.reshape(3, 3 * oc, cl)
    dma = pltpu.SemaphoreType.DMA
    return pl.pallas_call(
        functools.partial(kernel, n),
        out_shape=jax.ShapeDtypeStruct((rows // 4, lc, cl), BF16),
        in_specs=[pl.BlockSpec(memory_space=pl.ANY)] * 5,
        out_specs=pl.BlockSpec(memory_space=pltpu.VMEM),
        scratch_shapes=[
            pltpu.VMEM((rows + 4, cols, ch), BF16),
            pltpu.VMEM(first.shape, BF16),
            pltpu.VMEM(second.shape, BF16),
            pltpu.VMEM(weight_mix.shape, BF16),
            pltpu.VMEM(last.shape, BF16),
            pltpu.VMEM((2 * ch, lw // 2), BF16),
            pltpu.VMEM((gs * 16, gs * 16), BF16),
            pltpu.VMEM((gs * 16, gs * 16), BF16),
            pltpu.VMEM((2, n, 16, lw // 2), BF16),
            pltpu.VMEM((2, n * lc, cl // 2), BF16),
            pltpu.VMEM((2, 2, n // 2, 16, lw // 2), BF16),
            pltpu.VMEM((2, n // 2, 16, lw // 2), BF16),
            pltpu.VMEM((2, n // 2, 16, lw // 2), BF16),
            pltpu.VMEM((2, n // 2, 16, lw // 2), BF16),
            dma((4, 3)),
            dma,
            dma((2,)),
            dma((2,)),
            dma((2, n // 2)),
            dma((2, n // 2)),
            dma((2, n // 2)),
            dma((2, n // 2)),
            dma((2,)),
            dma((2,)),
            dma((2, n // 2)),
            dma((2, n // 2)),
        ],
        compiler_params=pltpu.CompilerParams(
            collective_id=0, has_side_effects=True, vmem_limit_bytes=56 * 1024 * 1024
        ),
    )(pixels, first, second, weight_mix, last)


def solution(mesh):
    return jax.shard_map(
        functools.partial(local, mesh.shape["rows"]),
        mesh=mesh,
        in_specs=(
            P(("groups", "rows"), None, None),
            P(),
            P(),
            P(None, None, None, "rows"),
            P(None, None, "rows", None),
        ),
        out_specs=P(("groups", "rows"), None, None),
        check_vma=False,
    )
```

```python
import functools

import jax
import jax.numpy as jnp
from jax import lax
from jax.experimental import pallas as pl
from jax.experimental.pallas import tpu as pltpu
from jax.sharding import PartitionSpec as P

MESH = pl.DeviceIdType.MESH
BF16 = jnp.bfloat16
F32 = jnp.float32


def quotient(value, divisor):
    if divisor & (divisor - 1) == 0:
        return lax.shift_right_logical(value, divisor.bit_length() - 1)
    return value // divisor


def remainder(value, divisor):
    if divisor & (divisor - 1) == 0:
        return value & (divisor - 1)
    return value % divisor


def index(shape, dim):
    return lax.broadcasted_iota(jnp.int32, shape, dim)


def selection(mask, entry):
    return jnp.where(mask, entry, 0.0).astype(BF16)


def dot(left, right):
    return jnp.dot(left, right, preferred_element_type=F32)


def silu(value):
    return value / (1.0 + jnp.exp(-value))


def column_taps(value, cols):
    length = value.shape[0]
    col = remainder(index(value.shape, 0), cols)
    left = jnp.where(col == 0, 0.0, pltpu.roll(value, 1, 0))
    right = jnp.where(col == cols - 1, 0.0, pltpu.roll(value, length - 1, 0))
    return jnp.concatenate([left.astype(BF16), value.astype(BF16), right.astype(BF16)], axis=1)


def latent_tap(value, tap, rows, cols):
    row_step, col_step = tap // 3 - 1, tap % 3 - 1
    step = row_step * cols + col_step
    if step == 0:
        return value
    length = rows * cols
    place = index(value.shape, 0)
    row, col = quotient(place, cols) + row_step, remainder(place, cols) + col_step
    inside = (row >= 0) & (row < rows) & (col >= 0) & (col < cols)
    return jnp.where(inside, pltpu.roll(value, (-step) % length, 0), 0.0)


def kernel(
    n, px, w1, w2, wm, wo, out,
    ext, w1v, w2v, wmv, wov, mix_sel, sort_sel, back_sel, gathered, latents, outgoing, swapped, paired, incoming,
    wsem, psem, hsend, hrecv, gsend, grecv, fsend, frecv, xsend, xrecv, ssend, srecv,
):
    me = lax.axis_index("rows")
    core, chip, chips = lax.rem(me, 2), lax.div(me, 2), n // 2
    sibling = me + 1 - 2 * core
    rows, cols, ch = px.shape
    oc = wmv.shape[-1]
    lc = cols // 4
    nk = 16 // lc
    lw = 4 * ch // nk
    cw = ch // nk
    gs = min(n, 16)
    span = gs * lc
    pos = n * lc
    hw = lw // 2

    def twin(off):
        return 2 * lax.rem(chip + off, chips) + core

    own_pixels = pltpu.make_async_copy(px, ext.at[pl.ds(2, rows)], psem)
    own_pixels.start()
    loads = []
    for which, (src, dst) in enumerate(((w1, w1v), (w2, w2v), (wm, wmv), (wo, wov))):
        loads.append([pltpu.make_async_copy(src.at[a], dst.at[a], wsem.at[which, a]) for a in range(3)])
    for load in loads[0] + loads[1]:
        load.start(priority=1)

    barrier = pltpu.get_barrier_semaphore()

    def greet(peer):
        pl.semaphore_signal(barrier, inc=1, device_id={"rows": peer}, device_id_type=MESH)

    def greet_chip(off, carry):
        greet(twin(off))
        return carry

    greet(lax.rem(jnp.where(core == 0, me + n - 1, me + 1), n))
    greet(sibling)
    lax.fori_loop(1, chips, greet_chip, 0)

    blank = jnp.zeros((2, cols, ch), BF16)

    @pl.when(me == 0)
    def _():
        ext[pl.ds(0, 2)] = blank

    @pl.when(me == n - 1)
    def _():
        ext[pl.ds(rows + 2, 2)] = blank

    pl.semaphore_wait(barrier, chips + 1)

    down = pltpu.make_async_remote_copy(
        src_ref=px.at[pl.ds(rows - 2, 2)], dst_ref=ext.at[pl.ds(0, 2)],
        send_sem=hsend.at[0], recv_sem=hrecv.at[0],
        device_id={"rows": lax.rem(me + 1, n)}, device_id_type=MESH,
    )
    up = pltpu.make_async_remote_copy(
        src_ref=px.at[pl.ds(0, 2)], dst_ref=ext.at[pl.ds(rows + 2, 2)],
        send_sem=hsend.at[1], recv_sem=hrecv.at[1],
        device_id={"rows": lax.rem(me + n - 1, n)}, device_id_type=MESH,
    )

    @pl.when(me < n - 1)
    def _():
        down.start()

    @pl.when(me > 0)
    def _():
        up.start()

    shape = (lw, lw)
    row, col = index(shape, 0), index(shape, 1)
    mix_sel[...] = selection(col == remainder(row, cw) * 4 + quotient(row, cw), 1.0)
    shape = (gs * 16, gs * 16)
    row, col = index(shape, 0), index(shape, 1)
    wanted = remainder(quotient(row, lc), gs) * 16 + quotient(row, span) * lc + remainder(row, lc)
    sort_sel[...] = selection(col == wanted, 1.0)
    place = quotient(row, 16)
    place = 2 * remainder(place, gs // 2) + quotient(place, gs // 2)
    wanted = remainder(quotient(row, lc), nk) * span + place * lc + remainder(row, lc)
    back_sel[...] = selection(col == wanted, 1.0)
    shape = (rows * cols // 2, rows * cols)
    pair_sel = selection(index(shape, 0) == quotient(index(shape, 1), 2), 0.5)
    shape = (64, rows * cols // 2)
    row, col = index(shape, 0), index(shape, 1)
    part = quotient(row, 16)
    strip = 2 * remainder(part, 2) + quotient(part, 2)
    quad_sel = selection(quotient(col, 2) == strip * lc + remainder(row, lc), 0.5)

    own_pixels.wait()

    @pl.when(me > 0)
    def _():
        down.wait_recv()

    @pl.when(me < n - 1)
    def _():
        up.wait_recv()

    for load in loads[2] + loads[3]:
        load.start(priority=1)

    pixels = ext[...].reshape((rows + 4) * cols, ch).astype(F32)
    taps = column_taps(pixels, cols)
    summed = jnp.zeros(((rows + 2) * cols, ch), F32)
    for a in range(3):
        loads[0][a].wait()
        summed = summed + dot(taps[a * cols : (a + rows + 2) * cols], w1v[a])
    row = quotient(index(summed.shape, 0), cols)
    outside = ((row == 0) & (me == 0)) | ((row == rows + 1) & (me == n - 1))
    activated = jnp.where(outside, 0.0, silu(summed)).astype(BF16)
    taps = column_taps(activated.astype(F32), cols)
    summed = pixels[2 * cols : (rows + 2) * cols]
    conv = jnp.zeros((rows * cols, ch), F32)
    for a in range(3):
        loads[1][a].wait()
        conv = conv + dot(taps[a * cols : (a + rows) * cols], w2v[a])
    block_out = (summed + conv).astype(BF16)

    half_res = dot(pair_sel, block_out).astype(BF16)
    quads = dot(quad_sel, half_res)
    chunk = quotient(index((16, cw), 0), lc)
    pieces = []
    for q in range(4):
        mine = quads[16 * q : 16 * q + 16]
        piece = mine[:, :cw]
        for k in range(1, nk):
            piece = jnp.where(chunk == k, mine[:, k * cw : (k + 1) * cw], piece)
        pieces.append(piece)
    latent = dot(jnp.concatenate(pieces, axis=1).astype(BF16), mix_sel[...]).astype(BF16)
    gathered[pl.ds(me, 1)] = latent[None]

    def handover(off):
        slot = gathered.at[twin(off)]
        return pltpu.make_async_remote_copy(
            src_ref=slot, dst_ref=slot, send_sem=fsend.at[off], recv_sem=frecv.at[off],
            device_id={"rows": sibling}, device_id_type=MESH,
        )

    def spread(off, slot):
        return pltpu.make_async_remote_copy(
            src_ref=gathered.at[slot], dst_ref=gathered.at[slot],
            send_sem=gsend.at[off], recv_sem=grecv.at[off],
            device_id={"rows": twin(off)}, device_id_type=MESH,
        )

    def push_latent(off, carry):
        spread(off, me).start()
        return carry

    def pass_on(off, carry):
        spread(off, twin(chips - off)).wait_recv()
        handover(chips - off).start()
        return carry

    def take_latent(off, carry):
        slot = gathered.at[2 * lax.rem(chip + off, chips) + 1 - core]
        pltpu.make_async_remote_copy(
            src_ref=slot, dst_ref=slot, send_sem=fsend.at[off], recv_sem=frecv.at[off],
            device_id={"rows": sibling}, device_id_type=MESH,
        ).wait_recv()
        return carry

    def settle_latent(off, carry):
        spread(off, me).wait_send()
        handover(off).wait_send()
        return carry

    lax.fori_loop(1, chips, push_latent, 0)
    handover(0).start()
    lax.fori_loop(1, chips, pass_on, 0)
    lax.fori_loop(0, chips, take_latent, 0)

    for g in range(n // gs):
        block = gathered[pl.ds(g * gs, gs)].reshape(gs * 16, lw)
        ordered = dot(sort_sel[...], block).astype(BF16)
        for k in range(nk):
            latents[pl.ds(g * span, span), pl.ds(k * lw, lw)] = ordered[k * span : (k + 1) * span]

    for load in loads[2]:
        load.wait()
    everywhere = latents[...]
    width = 2 if oc % 128 == 0 else 1
    hidden = jnp.zeros((pos, oc), F32)
    for first in range(0, 9, width):
        group = range(first, min(first + width, 9))
        weights = [wmv[tap // 3, tap % 3] for tap in group]
        weight = weights[0] if len(weights) == 1 else jnp.concatenate(weights, axis=1)
        terms = dot(everywhere, weight)
        for at, tap in enumerate(group):
            hidden = hidden + latent_tap(terms[:, at * oc : (at + 1) * oc], tap, n, lc)
    hidden = silu(hidden).astype(BF16).astype(F32)

    for load in loads[3]:
        load.wait()
    shifted = [latent_tap(hidden, tap, n, lc).astype(BF16) for tap in range(9)]
    if oc % 128 == 0:
        shifted = jnp.concatenate(shifted, axis=1)

    def contribution(start):
        lanes = pl.ds(start, hw)
        if oc % 128 == 0:
            return dot(shifted, wov[:, :, lanes].reshape(9 * oc, hw)).astype(BF16)
        total = jnp.zeros((pos, hw), F32)
        for tap in range(9):
            total = total + dot(shifted[tap], wov[tap // 3, pl.ds(tap % 3 * oc, oc), lanes])
        return total.astype(BF16)

    def swap(h):
        return pltpu.make_async_remote_copy(
            src_ref=outgoing.at[h, 1 - core], dst_ref=swapped.at[h],
            send_sem=xsend.at[h], recv_sem=xrecv.at[h],
            device_id={"rows": sibling}, device_id_type=MESH,
        )

    def scatter(h, off, slot):
        return pltpu.make_async_remote_copy(
            src_ref=paired.at[h, lax.rem(chip + off, chips)], dst_ref=incoming.at[h, slot],
            send_sem=ssend.at[h, off], recv_sem=srecv.at[h, off],
            device_id={"rows": twin(off)}, device_id_type=MESH,
        )

    def multiply(h):
        parts = [contribution((h * nk + k) * hw) for k in range(nk)]
        for g in range(n // gs):
            block = jnp.concatenate([part[g * span : (g + 1) * span] for part in parts], axis=0)
            block = dot(back_sel[...], block).astype(BF16).reshape(2, gs // 2, 16, hw)
            outgoing[h, :, pl.ds(g * gs // 2, gs // 2)] = block
        swap(h).start()

    def send_sums(h):
        swap(h).wait_recv()
        paired[h] = (outgoing[h, core].astype(F32) + swapped[h].astype(F32)).astype(BF16)

        def push_sum(off, carry):
            scatter(h, off, chip).start()
            return carry

        lax.fori_loop(1, chips, push_sum, 0)
        incoming[h, pl.ds(chip, 1)] = paired[h, pl.ds(chip, 1)]

    multiply(0)
    multiply(1)
    send_sums(0)
    send_sums(1)

    @pl.when(me < n - 1)
    def _():
        down.wait_send()

    @pl.when(me > 0)
    def _():
        up.wait_send()

    handover(0).wait_send()
    lax.fori_loop(1, chips, settle_latent, 0)
    residual = latent.astype(F32)
    for h in range(2):

        def take_sum(off, carry):
            scatter(h, off, lax.rem(chip + chips - off, chips)).wait_recv()
            return carry

        lax.fori_loop(1, chips, take_sum, 0)
        total = jnp.sum(incoming[h].astype(F32), axis=0)
        for k in range(nk):
            whole = h * nk + k
            piece = residual[whole // 2 * lc : (whole // 2 + 1) * lc, whole % 2 * hw : (whole % 2 + 1) * hw]
            out[0, :, pl.ds(whole * hw, hw)] = (total[k * lc : (k + 1) * lc] + piece).astype(BF16)

    for h in range(2):
        swap(h).wait_send()

        def settle_sum(off, carry):
            scatter(h, off, chip).wait_send()
            return carry

        lax.fori_loop(1, chips, settle_sum, 0)


def local(n, pixels, weight_first, weight_second, weight_mix, weight_out):
    rows, cols, ch = pixels.shape
    cl, oc = weight_mix.shape[2:]
    lc = cols // 4
    nk = 16 // lc
    lw = cl // nk
    gs = min(n, 16)
    first = weight_first.reshape(3, 3 * ch, ch)
    second = weight_second.reshape(3, 3 * ch, ch)
    last = weight_out.reshape(3, 3 * oc, cl)
    dma = pltpu.SemaphoreType.DMA
    return pl.pallas_call(
        functools.partial(kernel, n),
        out_shape=jax.ShapeDtypeStruct((rows // 4, lc, cl), BF16),
        in_specs=[pl.BlockSpec(memory_space=pl.ANY)] * 5,
        out_specs=pl.BlockSpec(memory_space=pltpu.VMEM),
        scratch_shapes=[
            pltpu.VMEM((rows + 4, cols, ch), BF16),
            pltpu.VMEM(first.shape, BF16),
            pltpu.VMEM(second.shape, BF16),
            pltpu.VMEM(weight_mix.shape, BF16),
            pltpu.VMEM(last.shape, BF16),
            pltpu.VMEM((lw, lw), BF16),
            pltpu.VMEM((gs * 16, gs * 16), BF16),
            pltpu.VMEM((gs * 16, gs * 16), BF16),
            pltpu.VMEM((n, 16, lw), BF16),
            pltpu.VMEM((n * lc, cl), BF16),
            pltpu.VMEM((2, 2, n // 2, 16, lw // 2), BF16),
            pltpu.VMEM((2, n // 2, 16, lw // 2), BF16),
            pltpu.VMEM((2, n // 2, 16, lw // 2), BF16),
            pltpu.VMEM((2, n // 2, 16, lw // 2), BF16),
            dma((4, 3)),
            dma,
            dma((2,)),
            dma((2,)),
            dma((n // 2,)),
            dma((n // 2,)),
            dma((n // 2,)),
            dma((n // 2,)),
            dma((2,)),
            dma((2,)),
            dma((2, n // 2)),
            dma((2, n // 2)),
        ],
        compiler_params=pltpu.CompilerParams(
            collective_id=0, has_side_effects=True, vmem_limit_bytes=56 * 1024 * 1024
        ),
    )(pixels, first, second, weight_mix, last)


def solution(mesh):
    return jax.shard_map(
        functools.partial(local, mesh.shape["rows"]),
        mesh=mesh,
        in_specs=(
            P(("groups", "rows"), None, None),
            P(),
            P(),
            P(None, None, None, "rows"),
            P(None, None, "rows", None),
        ),
        out_specs=P(("groups", "rows"), None, None),
        check_vma=False,
    )
```

```python
import functools

import jax
import jax.numpy as jnp
from jax import lax
from jax.experimental import pallas as pl
from jax.experimental.pallas import tpu as pltpu
from jax.sharding import PartitionSpec as P

MESH = pl.DeviceIdType.MESH
BF16 = jnp.bfloat16
F32 = jnp.float32


def quotient(value, divisor):
    if divisor & (divisor - 1) == 0:
        return lax.shift_right_logical(value, divisor.bit_length() - 1)
    return value // divisor


def remainder(value, divisor):
    if divisor & (divisor - 1) == 0:
        return value & (divisor - 1)
    return value % divisor


def index(shape, dim):
    return lax.broadcasted_iota(jnp.int32, shape, dim)


def selection(mask, entry):
    return jnp.where(mask, entry, 0.0).astype(BF16)


def dot(left, right):
    return jnp.dot(left, right, preferred_element_type=F32)


def silu(value):
    return value / (1.0 + jnp.exp(-value))


def column_taps(value, cols):
    length = value.shape[0]
    col = remainder(index(value.shape, 0), cols)
    left = jnp.where(col == 0, 0.0, pltpu.roll(value, 1, 0))
    right = jnp.where(col == cols - 1, 0.0, pltpu.roll(value, length - 1, 0))
    return jnp.concatenate([left.astype(BF16), value.astype(BF16), right.astype(BF16)], axis=1)


def latent_tap(value, tap, rows, cols):
    row_step, col_step = tap // 3 - 1, tap % 3 - 1
    step = row_step * cols + col_step
    if step == 0:
        return value
    length = rows * cols
    place = index(value.shape, 0)
    row, col = quotient(place, cols) + row_step, remainder(place, cols) + col_step
    inside = (row >= 0) & (row < rows) & (col >= 0) & (col < cols)
    return jnp.where(inside, pltpu.roll(value, (-step) % length, 0), 0.0)


def each(count, body):
    if count <= 16:
        for off in range(1, count):
            body(off)
        return

    def step(off, carry):
        body(off)
        return carry

    lax.fori_loop(1, count, step, 0)


def kernel(
    n, px, w1, w2, wm, wo, out,
    ext, w1v, w2v, wmv, wov, mix_sel, sort_sel, back_sel, gathered, latents, outgoing, swapped, paired, incoming,
    wsem, psem, hsend, hrecv, gsend, grecv, fsend, frecv, xsend, xrecv, ssend, srecv,
):
    me = lax.axis_index("rows")
    core, chip, chips = me & 1, lax.shift_right_logical(me, 1), n // 2
    sibling = me + 1 - 2 * core
    even = chips & (chips - 1) == 0
    rows, cols, ch = px.shape
    oc = wmv.shape[-1]
    lc = cols // 4
    nk = 16 // lc
    lw = 4 * ch // nk
    cw = ch // nk
    gs = min(n, 16)
    span = gs * lc
    pos = n * lc
    hw = lw // 2

    def chip_at(off):
        return chip ^ off if even else lax.rem(chip + off, chips)

    def twin(off):
        return 2 * chip_at(off) + core

    own_pixels = pltpu.make_async_copy(px, ext.at[pl.ds(2, rows)], psem)
    own_pixels.start()
    loads = []
    for which, (src, dst) in enumerate(((w1, w1v), (w2, w2v), (wm, wmv), (wo, wov))):
        loads.append([pltpu.make_async_copy(src.at[a], dst.at[a], wsem.at[which, a]) for a in range(3)])
    for load in loads[0] + loads[1]:
        load.start()

    barrier = pltpu.get_barrier_semaphore()

    def greet(peer):
        pl.semaphore_signal(barrier, inc=1, device_id={"rows": peer}, device_id_type=MESH)

    before, after = jnp.where(me == 0, n - 1, me - 1), jnp.where(me == n - 1, 0, me + 1)
    greet(jnp.where(core == 0, before, after))
    greet(sibling)
    each(chips, lambda off: greet(twin(off)))

    blank = jnp.zeros((2, cols, ch), BF16)

    @pl.when(me == 0)
    def _():
        ext[pl.ds(0, 2)] = blank

    @pl.when(me == n - 1)
    def _():
        ext[pl.ds(rows + 2, 2)] = blank

    pl.semaphore_wait(barrier, chips + 1)

    down = pltpu.make_async_remote_copy(
        src_ref=px.at[pl.ds(rows - 2, 2)], dst_ref=ext.at[pl.ds(0, 2)],
        send_sem=hsend.at[0], recv_sem=hrecv.at[0],
        device_id={"rows": after}, device_id_type=MESH,
    )
    up = pltpu.make_async_remote_copy(
        src_ref=px.at[pl.ds(0, 2)], dst_ref=ext.at[pl.ds(rows + 2, 2)],
        send_sem=hsend.at[1], recv_sem=hrecv.at[1],
        device_id={"rows": before}, device_id_type=MESH,
    )

    @pl.when(me < n - 1)
    def _():
        down.start()

    @pl.when(me > 0)
    def _():
        up.start()

    shape = (lw, lw)
    row, col = index(shape, 0), index(shape, 1)
    mix_sel[...] = selection(col == remainder(row, cw) * 4 + quotient(row, cw), 1.0)
    shape = (gs * 16, gs * 16)
    row, col = index(shape, 0), index(shape, 1)
    place = remainder(quotient(row, lc), gs)
    place = remainder(place, 2) * (gs // 2) + quotient(place, 2)
    wanted = place * 16 + quotient(row, span) * lc + remainder(row, lc)
    sort_sel[...] = selection(col == wanted, 1.0)
    place = quotient(row, 16)
    place = 2 * remainder(place, gs // 2) + quotient(place, gs // 2)
    wanted = remainder(quotient(row, lc), nk) * span + place * lc + remainder(row, lc)
    back_sel[...] = selection(col == wanted, 1.0)
    shape = (rows * cols // 2, rows * cols)
    pair_sel = selection(index(shape, 0) == quotient(index(shape, 1), 2), 0.5)
    shape = (64, rows * cols // 2)
    row, col = index(shape, 0), index(shape, 1)
    part = quotient(row, 16)
    strip = 2 * remainder(part, 2) + quotient(part, 2)
    quad_sel = selection(quotient(col, 2) == strip * lc + remainder(row, lc), 0.5)

    own_pixels.wait()

    @pl.when(me > 0)
    def _():
        down.wait_recv()

    @pl.when(me < n - 1)
    def _():
        up.wait_recv()

    for load in loads[2] + loads[3]:
        load.start()

    pixels = ext[...].reshape((rows + 4) * cols, ch).astype(F32)
    taps = column_taps(pixels, cols)
    summed = jnp.zeros(((rows + 2) * cols, ch), F32)
    for a in range(3):
        loads[0][a].wait()
        summed = summed + dot(taps[a * cols : (a + rows + 2) * cols], w1v[a])
    row = quotient(index(summed.shape, 0), cols)
    outside = ((row == 0) & (me == 0)) | ((row == rows + 1) & (me == n - 1))
    activated = jnp.where(outside, 0.0, silu(summed)).astype(BF16)
    taps = column_taps(activated.astype(F32), cols)
    summed = pixels[2 * cols : (rows + 2) * cols]
    conv = jnp.zeros((rows * cols, ch), F32)
    for a in range(3):
        loads[1][a].wait()
        conv = conv + dot(taps[a * cols : (a + rows) * cols], w2v[a])
    block_out = (summed + conv).astype(BF16)

    half_res = dot(pair_sel, block_out).astype(BF16)
    quads = dot(quad_sel, half_res)
    chunk = quotient(index((16, cw), 0), lc)
    pieces = []
    for q in range(4):
        mine = quads[16 * q : 16 * q + 16]
        piece = mine[:, :cw]
        for k in range(1, nk):
            piece = jnp.where(chunk == k, mine[:, k * cw : (k + 1) * cw], piece)
        pieces.append(piece)
    latent = dot(jnp.concatenate(pieces, axis=1).astype(BF16), mix_sel[...]).astype(BF16)
    gathered[core, pl.ds(chip, 1)] = latent[None]

    handover = pltpu.make_async_remote_copy(
        src_ref=gathered.at[core], dst_ref=gathered.at[core], send_sem=fsend, recv_sem=frecv,
        device_id={"rows": sibling}, device_id_type=MESH,
    )
    others = gathered.at[core, pl.ds(0, chips - 1)]
    spread = pltpu.make_async_remote_copy(
        src_ref=others, dst_ref=others, send_sem=gsend, recv_sem=grecv,
        device_id={"rows": sibling}, device_id_type=MESH,
    )

    def push_latent(off):
        slot = gathered.at[core, chip]
        pltpu.make_async_remote_copy(
            src_ref=slot, dst_ref=slot, send_sem=gsend, recv_sem=grecv,
            device_id={"rows": twin(off)}, device_id_type=MESH,
        ).start()

    each(chips, push_latent)
    if chips > 1:
        spread.wait_recv()
    handover.start()
    handover.wait_recv()

    for g in range(n // gs):
        block = gathered[:, pl.ds(g * gs // 2, gs // 2)].reshape(gs * 16, lw)
        ordered = dot(sort_sel[...], block).astype(BF16)
        for k in range(nk):
            latents[pl.ds(g * span, span), pl.ds(k * lw, lw)] = ordered[k * span : (k + 1) * span]

    for load in loads[2]:
        load.wait()
    everywhere = latents[...]
    width = 2 if oc % 128 == 0 else 1
    hidden = jnp.zeros((pos, oc), F32)
    for first in range(0, 9, width):
        group = range(first, min(first + width, 9))
        weights = [wmv[tap // 3, tap % 3] for tap in group]
        weight = weights[0] if len(weights) == 1 else jnp.concatenate(weights, axis=1)
        terms = dot(everywhere, weight)
        for at, tap in enumerate(group):
            hidden = hidden + latent_tap(terms[:, at * oc : (at + 1) * oc], tap, n, lc)
    hidden = silu(hidden).astype(BF16).astype(F32)

    for load in loads[3]:
        load.wait()
    shifted = [latent_tap(hidden, tap, n, lc).astype(BF16) for tap in range(9)]
    if oc % 128 == 0:
        shifted = jnp.concatenate(shifted, axis=1)

    def contribution(start):
        lanes = pl.ds(start, hw)
        if oc % 128 == 0:
            return dot(shifted, wov[:, :, lanes].reshape(9 * oc, hw)).astype(BF16)
        total = jnp.zeros((pos, hw), F32)
        for tap in range(9):
            total = total + dot(shifted[tap], wov[tap // 3, pl.ds(tap % 3 * oc, oc), lanes])
        return total.astype(BF16)

    def swap(h):
        return pltpu.make_async_remote_copy(
            src_ref=outgoing.at[h, 1 - core], dst_ref=swapped.at[h],
            send_sem=xsend.at[h], recv_sem=xrecv.at[h],
            device_id={"rows": sibling}, device_id_type=MESH,
        )

    def scatter(h):
        several = pl.ds(0, chips - 1)
        return pltpu.make_async_remote_copy(
            src_ref=paired.at[h, several], dst_ref=incoming.at[h, several],
            send_sem=ssend.at[h], recv_sem=srecv.at[h],
            device_id={"rows": sibling}, device_id_type=MESH,
        )

    def multiply(h):
        parts = [contribution((h * nk + k) * hw) for k in range(nk)]
        for g in range(n // gs):
            block = jnp.concatenate([part[g * span : (g + 1) * span] for part in parts], axis=0)
            block = dot(back_sel[...], block).astype(BF16).reshape(2, gs // 2, 16, hw)
            outgoing[h, :, pl.ds(g * gs // 2, gs // 2)] = block
        swap(h).start()

    def send_sums(h):
        swap(h).wait_recv()
        paired[h] = (outgoing[h, core].astype(F32) + swapped[h].astype(F32)).astype(BF16)

        def push_sum(off):
            pltpu.make_async_remote_copy(
                src_ref=paired.at[h, chip_at(off)], dst_ref=incoming.at[h, off],
                send_sem=ssend.at[h], recv_sem=srecv.at[h],
                device_id={"rows": twin(off)}, device_id_type=MESH,
            ).start()

        each(chips, push_sum)
        incoming[h, pl.ds(0, 1)] = paired[h, pl.ds(chip, 1)]

    multiply(0)
    multiply(1)
    send_sums(0)
    send_sums(1)

    @pl.when(me < n - 1)
    def _():
        down.wait_send()

    @pl.when(me > 0)
    def _():
        up.wait_send()

    handover.wait_send()
    if chips > 1:
        spread.wait_send()
    residual = latent.astype(F32)
    for h in range(2):
        if chips > 1:
            scatter(h).wait_recv()
        total = jnp.sum(incoming[h].astype(F32), axis=0)
        for k in range(nk):
            whole = h * nk + k
            piece = residual[whole // 2 * lc : (whole // 2 + 1) * lc, whole % 2 * hw : (whole % 2 + 1) * hw]
            out[0, :, pl.ds(whole * hw, hw)] = (total[k * lc : (k + 1) * lc] + piece).astype(BF16)

    for h in range(2):
        swap(h).wait_send()
        if chips > 1:
            scatter(h).wait_send()


def local(n, pixels, weight_first, weight_second, weight_mix, weight_out):
    rows, cols, ch = pixels.shape
    cl, oc = weight_mix.shape[2:]
    lc = cols // 4
    nk = 16 // lc
    lw = cl // nk
    gs = min(n, 16)
    first = weight_first.reshape(3, 3 * ch, ch)
    second = weight_second.reshape(3, 3 * ch, ch)
    last = weight_out.reshape(3, 3 * oc, cl)
    dma = pltpu.SemaphoreType.DMA
    return pl.pallas_call(
        functools.partial(kernel, n),
        out_shape=jax.ShapeDtypeStruct((rows // 4, lc, cl), BF16),
        in_specs=[pl.BlockSpec(memory_space=pl.ANY)] * 5,
        out_specs=pl.BlockSpec(memory_space=pltpu.VMEM),
        scratch_shapes=[
            pltpu.VMEM((rows + 4, cols, ch), BF16),
            pltpu.VMEM(first.shape, BF16),
            pltpu.VMEM(second.shape, BF16),
            pltpu.VMEM(weight_mix.shape, BF16),
            pltpu.VMEM(last.shape, BF16),
            pltpu.VMEM((lw, lw), BF16),
            pltpu.VMEM((gs * 16, gs * 16), BF16),
            pltpu.VMEM((gs * 16, gs * 16), BF16),
            pltpu.VMEM((2, n // 2, 16, lw), BF16),
            pltpu.VMEM((n * lc, cl), BF16),
            pltpu.VMEM((2, 2, n // 2, 16, lw // 2), BF16),
            pltpu.VMEM((2, n // 2, 16, lw // 2), BF16),
            pltpu.VMEM((2, n // 2, 16, lw // 2), BF16),
            pltpu.VMEM((2, n // 2, 16, lw // 2), BF16),
            dma((4, 3)),
            dma,
            dma((2,)),
            dma((2,)),
            dma,
            dma,
            dma,
            dma,
            dma((2,)),
            dma((2,)),
            dma((2,)),
            dma((2,)),
        ],
        compiler_params=pltpu.CompilerParams(
            collective_id=0, has_side_effects=True, vmem_limit_bytes=56 * 1024 * 1024
        ),
    )(pixels, first, second, weight_mix, last)


def solution(mesh):
    return jax.shard_map(
        functools.partial(local, mesh.shape["rows"]),
        mesh=mesh,
        in_specs=(
            P(("groups", "rows"), None, None),
            P(),
            P(),
            P(None, None, None, "rows"),
            P(None, None, "rows", None),
        ),
        out_specs=P(("groups", "rows"), None, None),
        check_vma=False,
    )
```

```python
import functools

import jax
import jax.numpy as jnp
from jax import lax
from jax.experimental import pallas as pl
from jax.experimental.pallas import tpu as pltpu
from jax.sharding import PartitionSpec as P

MESH = pl.DeviceIdType.MESH
BF16 = jnp.bfloat16
F32 = jnp.float32


def quotient(value, divisor):
    if divisor & (divisor - 1) == 0:
        return lax.shift_right_logical(value, divisor.bit_length() - 1)
    return value // divisor


def remainder(value, divisor):
    if divisor & (divisor - 1) == 0:
        return value & (divisor - 1)
    return value % divisor


def index(shape, dim):
    return lax.broadcasted_iota(jnp.int32, shape, dim)


def selection(mask, entry):
    return jnp.where(mask, entry, 0.0).astype(BF16)


def dot(left, right):
    return jnp.dot(left, right, preferred_element_type=F32)


def silu(value):
    return value / (1.0 + jnp.exp(-value))


def column_taps(value, cols):
    length = value.shape[0]
    col = remainder(index(value.shape, 0), cols)
    left = jnp.where(col == 0, 0.0, pltpu.roll(value, 1, 0))
    right = jnp.where(col == cols - 1, 0.0, pltpu.roll(value, length - 1, 0))
    return jnp.concatenate([left.astype(BF16), value.astype(BF16), right.astype(BF16)], axis=1)


def latent_tap(value, tap, rows, cols):
    row_step, col_step = tap // 3 - 1, tap % 3 - 1
    step = row_step * cols + col_step
    if step == 0:
        return value
    length = rows * cols
    place = index(value.shape, 0)
    row, col = quotient(place, cols) + row_step, remainder(place, cols) + col_step
    inside = (row >= 0) & (row < rows) & (col >= 0) & (col < cols)
    return jnp.where(inside, pltpu.roll(value, (-step) % length, 0), 0.0)


def each(count, body):
    if count <= 16:
        for off in range(1, count):
            body(off)
        return

    def step(off, carry):
        body(off)
        return carry

    lax.fori_loop(1, count, step, 0)


def kernel(
    n, px, w1, w2, wm, wo, out,
    ext, w1v, w2v, wmv, wov, mix_sel, sort_sel, back_sel, gathered, latents, outgoing, swapped, paired, incoming,
    wsem, psem, hsend, hrecv, gsend, grecv, fsend, frecv, xsend, xrecv, ssend, srecv,
):
    me = lax.axis_index("rows")
    core, chip, chips = me & 1, lax.shift_right_logical(me, 1), n // 2
    sibling = me + 1 - 2 * core
    even = chips & (chips - 1) == 0
    rows, cols, ch = px.shape
    oc = wmv.shape[-1]
    lc = cols // 4
    nk = 16 // lc
    lw = 4 * ch // nk
    cw = ch // nk
    gs = min(n, 16)
    span = gs * lc
    pos = n * lc
    hw = lw // 2

    def chip_at(off):
        return chip ^ off if even else lax.rem(chip + off, chips)

    def twin(off):
        return 2 * chip_at(off) + core

    own_pixels = pltpu.make_async_copy(px, ext.at[pl.ds(2, rows)], psem)
    own_pixels.start()
    loads = []
    for which, (src, dst) in enumerate(((w1, w1v), (w2, w2v), (wm, wmv), (wo, wov))):
        loads.append([])
        depth = src.shape[-2]
        pieces = 2 if depth % 32 == 0 else 1
        for a in range(3):
            for half in range(pieces):
                part = pl.ds(half * depth // pieces, depth // pieces)
                place = (a, slice(None), part) if len(src.shape) == 4 else (a, part)
                loads[-1].append(
                    pltpu.make_async_copy(src.at[place], dst.at[place], wsem.at[which, 2 * a + half])
                )

    def start_loads(which):
        for at, load in enumerate(loads[which]):
            load.start(priority=at % 2)

    start_loads(0)
    start_loads(1)

    barrier = pltpu.get_barrier_semaphore()

    def greet(peer):
        pl.semaphore_signal(barrier, inc=1, device_id={"rows": peer}, device_id_type=MESH)

    before, after = jnp.where(me == 0, n - 1, me - 1), jnp.where(me == n - 1, 0, me + 1)
    greet(jnp.where(core == 0, before, after))
    greet(sibling)
    each(chips, lambda off: greet(twin(off)))

    blank = jnp.zeros((2, cols, ch), BF16)

    @pl.when(me == 0)
    def _():
        ext[pl.ds(0, 2)] = blank

    @pl.when(me == n - 1)
    def _():
        ext[pl.ds(rows + 2, 2)] = blank

    pl.semaphore_wait(barrier, chips + 1)

    down = pltpu.make_async_remote_copy(
        src_ref=px.at[pl.ds(rows - 2, 2)], dst_ref=ext.at[pl.ds(0, 2)],
        send_sem=hsend.at[0], recv_sem=hrecv.at[0],
        device_id={"rows": after}, device_id_type=MESH,
    )
    up = pltpu.make_async_remote_copy(
        src_ref=px.at[pl.ds(0, 2)], dst_ref=ext.at[pl.ds(rows + 2, 2)],
        send_sem=hsend.at[1], recv_sem=hrecv.at[1],
        device_id={"rows": before}, device_id_type=MESH,
    )

    @pl.when(me < n - 1)
    def _():
        down.start()

    @pl.when(me > 0)
    def _():
        up.start()

    start_loads(2)
    start_loads(3)

    shape = (lw, lw)
    row, col = index(shape, 0), index(shape, 1)
    mix_sel[...] = selection(col == remainder(row, cw) * 4 + quotient(row, cw), 1.0)
    shape = (gs * 16, gs * 16)
    row, col = index(shape, 0), index(shape, 1)
    place = remainder(quotient(row, lc), gs)
    place = remainder(place, 2) * (gs // 2) + quotient(place, 2)
    wanted = place * 16 + quotient(row, span) * lc + remainder(row, lc)
    sort_sel[...] = selection(col == wanted, 1.0)
    place = quotient(row, 16)
    place = 2 * remainder(place, gs // 2) + quotient(place, gs // 2)
    wanted = remainder(quotient(row, lc), nk) * span + place * lc + remainder(row, lc)
    back_sel[...] = selection(col == wanted, 1.0)
    shape = (rows * cols // 2, rows * cols)
    pair_sel = selection(index(shape, 0) == quotient(index(shape, 1), 2), 0.5)
    shape = (64, rows * cols // 2)
    row, col = index(shape, 0), index(shape, 1)
    part = quotient(row, 16)
    strip = 2 * remainder(part, 2) + quotient(part, 2)
    quad_sel = selection(quotient(col, 2) == strip * lc + remainder(row, lc), 0.5)

    own_pixels.wait()

    @pl.when(me > 0)
    def _():
        down.wait_recv()

    @pl.when(me < n - 1)
    def _():
        up.wait_recv()

    pixels = ext[...].reshape((rows + 4) * cols, ch).astype(F32)
    taps = column_taps(pixels, cols)
    summed = jnp.zeros(((rows + 2) * cols, ch), F32)
    for a in range(3):
        for load in loads[0][a * len(loads[0]) // 3 : (a + 1) * len(loads[0]) // 3]:
            load.wait()
        summed = summed + dot(taps[a * cols : (a + rows + 2) * cols], w1v[a])
    row = quotient(index(summed.shape, 0), cols)
    outside = ((row == 0) & (me == 0)) | ((row == rows + 1) & (me == n - 1))
    activated = jnp.where(outside, 0.0, silu(summed)).astype(BF16)
    taps = column_taps(activated.astype(F32), cols)
    summed = pixels[2 * cols : (rows + 2) * cols]
    conv = jnp.zeros((rows * cols, ch), F32)
    for a in range(3):
        for load in loads[1][a * len(loads[1]) // 3 : (a + 1) * len(loads[1]) // 3]:
            load.wait()
        conv = conv + dot(taps[a * cols : (a + rows) * cols], w2v[a])
    block_out = (summed + conv).astype(BF16)

    half_res = dot(pair_sel, block_out).astype(BF16)
    quads = dot(quad_sel, half_res)
    chunk = quotient(index((16, cw), 0), lc)
    pieces = []
    for q in range(4):
        mine = quads[16 * q : 16 * q + 16]
        piece = mine[:, :cw]
        for k in range(1, nk):
            piece = jnp.where(chunk == k, mine[:, k * cw : (k + 1) * cw], piece)
        pieces.append(piece)
    latent = dot(jnp.concatenate(pieces, axis=1).astype(BF16), mix_sel[...]).astype(BF16)
    gathered[core, pl.ds(chip, 1)] = latent[None]

    handover = pltpu.make_async_remote_copy(
        src_ref=gathered.at[core], dst_ref=gathered.at[core], send_sem=fsend, recv_sem=frecv,
        device_id={"rows": sibling}, device_id_type=MESH,
    )
    others = gathered.at[core, pl.ds(0, chips - 1)]
    spread = pltpu.make_async_remote_copy(
        src_ref=others, dst_ref=others, send_sem=gsend, recv_sem=grecv,
        device_id={"rows": sibling}, device_id_type=MESH,
    )

    def push_latent(off):
        slot = gathered.at[core, chip]
        pltpu.make_async_remote_copy(
            src_ref=slot, dst_ref=slot, send_sem=gsend, recv_sem=grecv,
            device_id={"rows": twin(off)}, device_id_type=MESH,
        ).start()

    each(chips, push_latent)
    if chips > 1:
        spread.wait_recv()
    handover.start()
    handover.wait_recv()

    for g in range(n // gs):
        block = gathered[:, pl.ds(g * gs // 2, gs // 2)].reshape(gs * 16, lw)
        ordered = dot(sort_sel[...], block).astype(BF16)
        for k in range(nk):
            latents[pl.ds(g * span, span), pl.ds(k * lw, lw)] = ordered[k * span : (k + 1) * span]

    for load in loads[2]:
        load.wait()
    everywhere = latents[...]
    width = 2 if oc % 128 == 0 else 1
    hidden = jnp.zeros((pos, oc), F32)
    for first in range(0, 9, width):
        group = range(first, min(first + width, 9))
        weights = [wmv[tap // 3, tap % 3] for tap in group]
        weight = weights[0] if len(weights) == 1 else jnp.concatenate(weights, axis=1)
        terms = dot(everywhere, weight)
        for at, tap in enumerate(group):
            hidden = hidden + latent_tap(terms[:, at * oc : (at + 1) * oc], tap, n, lc)
    hidden = silu(hidden).astype(BF16).astype(F32)

    for load in loads[3]:
        load.wait()
    shifted = [latent_tap(hidden, tap, n, lc).astype(BF16) for tap in range(9)]
    if oc % 128 == 0:
        shifted = jnp.concatenate(shifted, axis=1)

    def contribution(start):
        lanes = pl.ds(start, hw)
        if oc % 128 == 0:
            return dot(shifted, wov[:, :, lanes].reshape(9 * oc, hw)).astype(BF16)
        total = jnp.zeros((pos, hw), F32)
        for tap in range(9):
            total = total + dot(shifted[tap], wov[tap // 3, pl.ds(tap % 3 * oc, oc), lanes])
        return total.astype(BF16)

    def swap(h):
        return pltpu.make_async_remote_copy(
            src_ref=outgoing.at[h, 1 - core], dst_ref=swapped.at[h],
            send_sem=xsend.at[h], recv_sem=xrecv.at[h],
            device_id={"rows": sibling}, device_id_type=MESH,
        )

    def scatter(h):
        several = pl.ds(0, chips - 1)
        return pltpu.make_async_remote_copy(
            src_ref=paired.at[h, several], dst_ref=incoming.at[h, several],
            send_sem=ssend.at[h], recv_sem=srecv.at[h],
            device_id={"rows": sibling}, device_id_type=MESH,
        )

    def multiply(h):
        parts = [contribution((h * nk + k) * hw) for k in range(nk)]
        for g in range(n // gs):
            block = jnp.concatenate([part[g * span : (g + 1) * span] for part in parts], axis=0)
            block = dot(back_sel[...], block).astype(BF16).reshape(2, gs // 2, 16, hw)
            outgoing[h, :, pl.ds(g * gs // 2, gs // 2)] = block
        swap(h).start()

    def send_sums(h):
        swap(h).wait_recv()
        paired[h] = (outgoing[h, core].astype(F32) + swapped[h].astype(F32)).astype(BF16)

        def push_sum(off):
            pltpu.make_async_remote_copy(
                src_ref=paired.at[h, chip_at(off)], dst_ref=incoming.at[h, off],
                send_sem=ssend.at[h], recv_sem=srecv.at[h],
                device_id={"rows": twin(off)}, device_id_type=MESH,
            ).start()

        each(chips, push_sum)
        incoming[h, pl.ds(0, 1)] = paired[h, pl.ds(chip, 1)]

    multiply(0)
    multiply(1)
    send_sums(0)
    send_sums(1)

    @pl.when(me < n - 1)
    def _():
        down.wait_send()

    @pl.when(me > 0)
    def _():
        up.wait_send()

    handover.wait_send()
    if chips > 1:
        spread.wait_send()
    residual = latent.astype(F32)
    for h in range(2):
        if chips > 1:
            scatter(h).wait_recv()
        total = jnp.sum(incoming[h].astype(F32), axis=0)
        for k in range(nk):
            whole = h * nk + k
            piece = residual[whole // 2 * lc : (whole // 2 + 1) * lc, whole % 2 * hw : (whole % 2 + 1) * hw]
            out[0, :, pl.ds(whole * hw, hw)] = (total[k * lc : (k + 1) * lc] + piece).astype(BF16)

    for h in range(2):
        swap(h).wait_send()
        if chips > 1:
            scatter(h).wait_send()


def local(n, pixels, weight_first, weight_second, weight_mix, weight_out):
    rows, cols, ch = pixels.shape
    cl, oc = weight_mix.shape[2:]
    lc = cols // 4
    nk = 16 // lc
    lw = cl // nk
    gs = min(n, 16)
    first = weight_first.reshape(3, 3 * ch, ch)
    second = weight_second.reshape(3, 3 * ch, ch)
    last = weight_out.reshape(3, 3 * oc, cl)
    dma = pltpu.SemaphoreType.DMA
    return pl.pallas_call(
        functools.partial(kernel, n),
        out_shape=jax.ShapeDtypeStruct((rows // 4, lc, cl), BF16),
        in_specs=[pl.BlockSpec(memory_space=pl.ANY)] * 5,
        out_specs=pl.BlockSpec(memory_space=pltpu.VMEM),
        scratch_shapes=[
            pltpu.VMEM((rows + 4, cols, ch), BF16),
            pltpu.VMEM(first.shape, BF16),
            pltpu.VMEM(second.shape, BF16),
            pltpu.VMEM(weight_mix.shape, BF16),
            pltpu.VMEM(last.shape, BF16),
            pltpu.VMEM((lw, lw), BF16),
            pltpu.VMEM((gs * 16, gs * 16), BF16),
            pltpu.VMEM((gs * 16, gs * 16), BF16),
            pltpu.VMEM((2, n // 2, 16, lw), BF16),
            pltpu.VMEM((n * lc, cl), BF16),
            pltpu.VMEM((2, 2, n // 2, 16, lw // 2), BF16),
            pltpu.VMEM((2, n // 2, 16, lw // 2), BF16),
            pltpu.VMEM((2, n // 2, 16, lw // 2), BF16),
            pltpu.VMEM((2, n // 2, 16, lw // 2), BF16),
            dma((4, 6)),
            dma,
            dma((2,)),
            dma((2,)),
            dma,
            dma,
            dma,
            dma,
            dma((2,)),
            dma((2,)),
            dma((2,)),
            dma((2,)),
        ],
        compiler_params=pltpu.CompilerParams(
            collective_id=0, has_side_effects=True, vmem_limit_bytes=56 * 1024 * 1024
        ),
    )(pixels, first, second, weight_mix, last)


def solution(mesh):
    return jax.shard_map(
        functools.partial(local, mesh.shape["rows"]),
        mesh=mesh,
        in_specs=(
            P(("groups", "rows"), None, None),
            P(),
            P(),
            P(None, None, None, "rows"),
            P(None, None, "rows", None),
        ),
        out_specs=P(("groups", "rows"), None, None),
        check_vma=False,
    )
```

```python
import functools

import jax
import jax.numpy as jnp
from jax import lax
from jax.experimental import pallas as pl
from jax.experimental.pallas import tpu as pltpu
from jax.sharding import PartitionSpec as P

MESH = pl.DeviceIdType.MESH
BF16 = jnp.bfloat16
F32 = jnp.float32


def quotient(value, divisor):
    if divisor & (divisor - 1) == 0:
        return lax.shift_right_logical(value, divisor.bit_length() - 1)
    return value // divisor


def remainder(value, divisor):
    if divisor & (divisor - 1) == 0:
        return value & (divisor - 1)
    return value % divisor


def index(shape, dim):
    return lax.broadcasted_iota(jnp.int32, shape, dim)


def selection(mask, entry):
    return jnp.where(mask, entry, 0.0).astype(BF16)


def dot(left, right):
    return jnp.dot(left, right, preferred_element_type=F32)


def silu(value):
    return value / (1.0 + jnp.exp(-value))


def column_taps(value, cols):
    length = value.shape[0]
    col = remainder(index(value.shape, 0), cols)
    left = jnp.where(col == 0, 0.0, pltpu.roll(value, 1, 0))
    right = jnp.where(col == cols - 1, 0.0, pltpu.roll(value, length - 1, 0))
    return jnp.concatenate([left.astype(BF16), value.astype(BF16), right.astype(BF16)], axis=1)


def latent_tap(value, tap, rows, cols):
    row_step, col_step = tap // 3 - 1, tap % 3 - 1
    step = row_step * cols + col_step
    if step == 0:
        return value
    length = rows * cols
    place = index(value.shape, 0)
    row, col = quotient(place, cols) + row_step, remainder(place, cols) + col_step
    inside = (row >= 0) & (row < rows) & (col >= 0) & (col < cols)
    return jnp.where(inside, pltpu.roll(value, (-step) % length, 0), 0.0)


def each(count, body):
    if count <= 16:
        for off in range(1, count):
            body(off)
        return

    def step(off, carry):
        body(off)
        return carry

    lax.fori_loop(1, count, step, 0)


def kernel(
    n, px, w1, w2, wm, wo, out,
    ext, w1v, w2v, wmv, wov, mix_sel, sort_sel, back_sel, gathered, latents, outgoing, swapped, paired, incoming,
    wsem, psem, hsend, hrecv, gsend, grecv, fsend, frecv, xsend, xrecv, ssend, srecv,
):
    me = lax.axis_index("rows")
    core, chip, chips = me & 1, lax.shift_right_logical(me, 1), n // 2
    sibling = me + 1 - 2 * core
    even = chips & (chips - 1) == 0
    rows, cols, ch = px.shape
    oc = wmv.shape[-1]
    lc = cols // 4
    nk = 16 // lc
    lw = 4 * ch // nk
    cw = ch // (2 * nk)
    gs = min(n, 16)
    span = gs * lc
    pos = n * lc
    hw = lw // 2

    def chip_at(off):
        return chip ^ off if even else lax.rem(chip + off, chips)

    def twin(off):
        return 2 * chip_at(off) + core

    own_pixels = pltpu.make_async_copy(px, ext.at[pl.ds(2, rows)], psem)
    own_pixels.start()
    loads = []
    for which, (src, dst) in enumerate(((w1, w1v), (w2, w2v), (wm, wmv), (wo, wov))):
        loads.append([pltpu.make_async_copy(src.at[a], dst.at[a], wsem.at[which, a]) for a in range(3)])
    for load in loads[0] + loads[1]:
        load.start()

    barrier = pltpu.get_barrier_semaphore()

    def greet(peer):
        pl.semaphore_signal(barrier, inc=1, device_id={"rows": peer}, device_id_type=MESH)

    before, after = jnp.where(me == 0, n - 1, me - 1), jnp.where(me == n - 1, 0, me + 1)
    greet(jnp.where(core == 0, before, after))
    greet(sibling)
    each(chips, lambda off: greet(twin(off)))

    blank = jnp.zeros((2, cols, ch), BF16)

    @pl.when(me == 0)
    def _():
        ext[pl.ds(0, 2)] = blank

    @pl.when(me == n - 1)
    def _():
        ext[pl.ds(rows + 2, 2)] = blank

    pl.semaphore_wait(barrier, chips + 1)

    down = pltpu.make_async_remote_copy(
        src_ref=px.at[pl.ds(rows - 2, 2)], dst_ref=ext.at[pl.ds(0, 2)],
        send_sem=hsend.at[0], recv_sem=hrecv.at[0],
        device_id={"rows": after}, device_id_type=MESH,
    )
    up = pltpu.make_async_remote_copy(
        src_ref=px.at[pl.ds(0, 2)], dst_ref=ext.at[pl.ds(rows + 2, 2)],
        send_sem=hsend.at[1], recv_sem=hrecv.at[1],
        device_id={"rows": before}, device_id_type=MESH,
    )

    @pl.when(me < n - 1)
    def _():
        down.start()

    @pl.when(me > 0)
    def _():
        up.start()

    shape = (2 * ch, hw)
    row, col = index(shape, 0), index(shape, 1)
    mix_sel[...] = selection(col == remainder(row, cw) * 4 + quotient(row, ch // 2), 1.0)
    shape = (rows * cols // 2, rows * cols)
    pair_sel = selection(index(shape, 0) == quotient(index(shape, 1), 2), 0.5)
    shape = (64, rows * cols // 2)
    row, col = index(shape, 0), index(shape, 1)
    part = quotient(row, 16)
    strip = 2 * remainder(part, 2) + quotient(part, 2)
    quad_sel = selection(quotient(col, 2) == strip * lc + remainder(row, lc), 0.5)

    own_pixels.wait()

    @pl.when(me > 0)
    def _():
        down.wait_recv()

    @pl.when(me < n - 1)
    def _():
        up.wait_recv()

    for load in loads[2] + loads[3]:
        load.start()

    pixels = ext[...].reshape((rows + 4) * cols, ch).astype(F32)
    taps = column_taps(pixels, cols)
    summed = jnp.zeros(((rows + 2) * cols, ch), F32)
    for a in range(3):
        loads[0][a].wait()
        summed = summed + dot(taps[a * cols : (a + rows + 2) * cols], w1v[a])
    row = quotient(index(summed.shape, 0), cols)
    outside = ((row == 0) & (me == 0)) | ((row == rows + 1) & (me == n - 1))
    activated = jnp.where(outside, 0.0, silu(summed)).astype(BF16)
    taps = column_taps(activated.astype(F32), cols)
    own = pixels[2 * cols : (rows + 2) * cols]
    for load in loads[1]:
        load.wait()
    chunk = quotient(index((16, ch // 2), 0), lc) == quotient(index((16, ch // 2), 1), cw)

    def make_latent(h):
        lanes = slice(h * ch // 2, (h + 1) * ch // 2)
        conv = dot(taps[: rows * cols], w2v[0, :, lanes])
        for a in range(1, 3):
            conv = conv + dot(taps[a * cols : (a + rows) * cols], w2v[a, :, lanes])
        block_out = (own[:, lanes] + conv).astype(BF16)
        half_res = dot(pair_sel, block_out).astype(BF16)
        quads = dot(quad_sel, half_res)
        pieces = [jnp.where(chunk, quads[16 * q : 16 * q + 16], 0.0).astype(BF16) for q in range(4)]
        return dot(jnp.concatenate(pieces, axis=1), mix_sel[...]).astype(BF16)

    def handover(h):
        return pltpu.make_async_remote_copy(
            src_ref=gathered.at[h, core], dst_ref=gathered.at[h, core],
            send_sem=fsend.at[h], recv_sem=frecv.at[h],
            device_id={"rows": sibling}, device_id_type=MESH,
        )

    def spread(h):
        others = gathered.at[h, core, pl.ds(0, chips - 1)]
        return pltpu.make_async_remote_copy(
            src_ref=others, dst_ref=others, send_sem=gsend.at[h], recv_sem=grecv.at[h],
            device_id={"rows": sibling}, device_id_type=MESH,
        )

    own_latents = []
    for h in range(2):
        own_latents.append(make_latent(h))
        gathered[h, core, pl.ds(chip, 1)] = own_latents[h][None]
        slot = gathered.at[h, core, chip]

        def push_latent(off):
            pltpu.make_async_remote_copy(
                src_ref=slot, dst_ref=slot, send_sem=gsend.at[h], recv_sem=grecv.at[h],
                device_id={"rows": twin(off)}, device_id_type=MESH,
            ).start()

        each(chips, push_latent)

    shape = (gs * 16, gs * 16)
    row, col = index(shape, 0), index(shape, 1)
    place = remainder(quotient(row, lc), gs)
    place = remainder(place, 2) * (gs // 2) + quotient(place, 2)
    wanted = place * 16 + quotient(row, span) * lc + remainder(row, lc)
    sort_sel[...] = selection(col == wanted, 1.0)
    place = quotient(row, 16)
    place = 2 * remainder(place, gs // 2) + quotient(place, gs // 2)
    wanted = remainder(quotient(row, lc), nk) * span + place * lc + remainder(row, lc)
    back_sel[...] = selection(col == wanted, 1.0)
    for load in loads[2]:
        load.wait()
    for h in range(2):
        if chips > 1:
            spread(h).wait_recv()
        handover(h).start()

    width = 2 if oc % 128 == 0 else 1
    groups = [range(first, min(first + width, 9)) for first in range(0, 9, width)]
    terms = [None] * len(groups)
    for h in range(2):
        handover(h).wait_recv()
        for g in range(n // gs):
            block = gathered[h, :, pl.ds(g * gs // 2, gs // 2)].reshape(gs * 16, hw)
            ordered = dot(sort_sel[...], block).astype(BF16)
            for k in range(nk):
                latents[h, pl.ds(g * span, span), pl.ds(k * hw, hw)] = ordered[k * span : (k + 1) * span]
        everywhere = latents[h]
        for at, group in enumerate(groups):
            weights = [wmv[tap // 3, tap % 3, pl.ds(h * nk * hw, nk * hw)] for tap in group]
            weight = weights[0] if len(weights) == 1 else jnp.concatenate(weights, axis=1)
            term = dot(everywhere, weight)
            terms[at] = term if h == 0 else terms[at] + term
    hidden = jnp.zeros((pos, oc), F32)
    for term, group in zip(terms, groups):
        for at, tap in enumerate(group):
            hidden = hidden + latent_tap(term[:, at * oc : (at + 1) * oc], tap, n, lc)
    hidden = silu(hidden).astype(BF16).astype(F32)

    for load in loads[3]:
        load.wait()
    shifted = [latent_tap(hidden, tap, n, lc).astype(BF16) for tap in range(9)]
    if oc % 128 == 0:
        shifted = jnp.concatenate(shifted, axis=1)

    def contribution(start):
        lanes = pl.ds(start, hw)
        if oc % 128 == 0:
            return dot(shifted, wov[:, :, lanes].reshape(9 * oc, hw)).astype(BF16)
        total = jnp.zeros((pos, hw), F32)
        for tap in range(9):
            total = total + dot(shifted[tap], wov[tap // 3, pl.ds(tap % 3 * oc, oc), lanes])
        return total.astype(BF16)

    def swap(h):
        return pltpu.make_async_remote_copy(
            src_ref=outgoing.at[h, 1 - core], dst_ref=swapped.at[h],
            send_sem=xsend.at[h], recv_sem=xrecv.at[h],
            device_id={"rows": sibling}, device_id_type=MESH,
        )

    def scatter(h):
        several = pl.ds(0, chips - 1)
        return pltpu.make_async_remote_copy(
            src_ref=paired.at[h, several], dst_ref=incoming.at[h, several],
            send_sem=ssend.at[h], recv_sem=srecv.at[h],
            device_id={"rows": sibling}, device_id_type=MESH,
        )

    def multiply(h):
        parts = [contribution((h * nk + k) * hw) for k in range(nk)]
        for g in range(n // gs):
            block = jnp.concatenate([part[g * span : (g + 1) * span] for part in parts], axis=0)
            block = dot(back_sel[...], block).astype(BF16).reshape(2, gs // 2, 16, hw)
            outgoing[h, :, pl.ds(g * gs // 2, gs // 2)] = block
        swap(h).start()

    def send_sums(h):
        swap(h).wait_recv()
        paired[h] = (outgoing[h, core].astype(F32) + swapped[h].astype(F32)).astype(BF16)

        def push_sum(off):
            pltpu.make_async_remote_copy(
                src_ref=paired.at[h, chip_at(off)], dst_ref=incoming.at[h, off],
                send_sem=ssend.at[h], recv_sem=srecv.at[h],
                device_id={"rows": twin(off)}, device_id_type=MESH,
            ).start()

        each(chips, push_sum)
        incoming[h, pl.ds(0, 1)] = paired[h, pl.ds(chip, 1)]

    multiply(0)
    multiply(1)
    send_sums(0)
    send_sums(1)

    @pl.when(me < n - 1)
    def _():
        down.wait_send()

    @pl.when(me > 0)
    def _():
        up.wait_send()

    for h in range(2):
        handover(h).wait_send()
        if chips > 1:
            spread(h).wait_send()
    for h in range(2):
        if chips > 1:
            scatter(h).wait_recv()
        total = jnp.sum(incoming[h].astype(F32), axis=0) + own_latents[h].astype(F32)
        for k in range(nk):
            out[0, :, pl.ds((h * nk + k) * hw, hw)] = total[k * lc : (k + 1) * lc].astype(BF16)

    for h in range(2):
        swap(h).wait_send()
        if chips > 1:
            scatter(h).wait_send()


def local(n, pixels, weight_first, weight_second, weight_mix, weight_out):
    rows, cols, ch = pixels.shape
    cl, oc = weight_mix.shape[2:]
    lc = cols // 4
    nk = 16 // lc
    lw = cl // nk
    gs = min(n, 16)
    first = weight_first.reshape(3, 3 * ch, ch)
    second = weight_second.reshape(3, 3 * ch, ch)
    last = weight_out.reshape(3, 3 * oc, cl)
    dma = pltpu.SemaphoreType.DMA
    return pl.pallas_call(
        functools.partial(kernel, n),
        out_shape=jax.ShapeDtypeStruct((rows // 4, lc, cl), BF16),
        in_specs=[pl.BlockSpec(memory_space=pl.ANY)] * 5,
        out_specs=pl.BlockSpec(memory_space=pltpu.VMEM),
        scratch_shapes=[
            pltpu.VMEM((rows + 4, cols, ch), BF16),
            pltpu.VMEM(first.shape, BF16),
            pltpu.VMEM(second.shape, BF16),
            pltpu.VMEM(weight_mix.shape, BF16),
            pltpu.VMEM(last.shape, BF16),
            pltpu.VMEM((2 * ch, lw // 2), BF16),
            pltpu.VMEM((gs * 16, gs * 16), BF16),
            pltpu.VMEM((gs * 16, gs * 16), BF16),
            pltpu.VMEM((2, 2, n // 2, 16, lw // 2), BF16),
            pltpu.VMEM((2, n * lc, cl // 2), BF16),
            pltpu.VMEM((2, 2, n // 2, 16, lw // 2), BF16),
            pltpu.VMEM((2, n // 2, 16, lw // 2), BF16),
            pltpu.VMEM((2, n // 2, 16, lw // 2), BF16),
            pltpu.VMEM((2, n // 2, 16, lw // 2), BF16),
            dma((4, 3)),
            dma,
            dma((2,)),
            dma((2,)),
            dma((2,)),
            dma((2,)),
            dma((2,)),
            dma((2,)),
            dma((2,)),
            dma((2,)),
            dma((2,)),
            dma((2,)),
        ],
        compiler_params=pltpu.CompilerParams(
            collective_id=0, has_side_effects=True, vmem_limit_bytes=56 * 1024 * 1024
        ),
    )(pixels, first, second, weight_mix, last)


def solution(mesh):
    return jax.shard_map(
        functools.partial(local, mesh.shape["rows"]),
        mesh=mesh,
        in_specs=(
            P(("groups", "rows"), None, None),
            P(),
            P(),
            P(None, None, None, "rows"),
            P(None, None, "rows", None),
        ),
        out_specs=P(("groups", "rows"), None, None),
        check_vma=False,
    )
```

```python
import functools

import jax
import jax.numpy as jnp
from jax import lax
from jax.experimental import pallas as pl
from jax.experimental.pallas import tpu as pltpu
from jax.sharding import PartitionSpec as P

MESH = pl.DeviceIdType.MESH
BF16 = jnp.bfloat16
F32 = jnp.float32


def quotient(value, divisor):
    if divisor & (divisor - 1) == 0:
        return lax.shift_right_logical(value, divisor.bit_length() - 1)
    return value // divisor


def remainder(value, divisor):
    if divisor & (divisor - 1) == 0:
        return value & (divisor - 1)
    return value % divisor


def index(shape, dim):
    return lax.broadcasted_iota(jnp.int32, shape, dim)


def selection(mask, entry):
    return jnp.where(mask, entry, 0.0).astype(BF16)


def dot(left, right):
    return jnp.dot(left, right, preferred_element_type=F32)


def silu(value):
    return value / (1.0 + jnp.exp(-value))


def column_taps(value, cols):
    length = value.shape[0]
    col = remainder(index(value.shape, 0), cols)
    left = jnp.where(col == 0, 0.0, pltpu.roll(value, 1, 0))
    right = jnp.where(col == cols - 1, 0.0, pltpu.roll(value, length - 1, 0))
    return jnp.concatenate([left.astype(BF16), value.astype(BF16), right.astype(BF16)], axis=1)


def latent_tap(value, tap, rows, cols):
    row_step, col_step = tap // 3 - 1, tap % 3 - 1
    step = row_step * cols + col_step
    if step == 0:
        return value
    length = rows * cols
    place = index(value.shape, 0)
    row, col = quotient(place, cols) + row_step, remainder(place, cols) + col_step
    inside = (row >= 0) & (row < rows) & (col >= 0) & (col < cols)
    return jnp.where(inside, pltpu.roll(value, (-step) % length, 0), 0.0)


def each(count, body):
    if count <= 16:
        for off in range(1, count):
            body(off)
        return

    def step(off, carry):
        body(off)
        return carry

    lax.fori_loop(1, count, step, 0)


def kernel(
    n, px, w1, w2, wm, wo, out,
    ext, w1v, w2v, wmv, wov, mix_sel, sort_sel, back_sel, gathered, latents, outgoing, swapped, paired, incoming, result,
    wsem, psem, hsend, hrecv, gsend, grecv, fsend, frecv, xsend, xrecv, ssend, srecv,
):
    me = lax.axis_index("rows")
    core, chip, chips = me & 1, lax.shift_right_logical(me, 1), n // 2
    sibling = me + 1 - 2 * core
    even = chips & (chips - 1) == 0
    rows, cols, ch = px.shape
    oc = wmv.shape[-1]
    lc = cols // 4
    nk = 16 // lc
    lw = 4 * ch // nk
    cw = ch // (2 * nk)
    gs = min(n, 16)
    span = gs * lc
    pos = n * lc
    hw = lw // 2

    def chip_at(off):
        return chip ^ off if even else lax.rem(chip + off, chips)

    def twin(off):
        return 2 * chip_at(off) + core

    own_pixels = pltpu.make_async_copy(px, ext.at[pl.ds(2, rows)], psem)
    own_pixels.start()
    loads = []
    for which, (src, dst) in enumerate(((w1, w1v), (w2, w2v), (wm, wmv), (wo, wov))):
        loads.append([pltpu.make_async_copy(src.at[a], dst.at[a], wsem.at[which, a]) for a in range(3)])
    for load in loads[0] + loads[1]:
        load.start()

    barrier = pltpu.get_barrier_semaphore()

    def greet(peer):
        pl.semaphore_signal(barrier, inc=1, device_id={"rows": peer}, device_id_type=MESH)

    before, after = jnp.where(me == 0, n - 1, me - 1), jnp.where(me == n - 1, 0, me + 1)
    greet(jnp.where(core == 0, before, after))
    greet(sibling)
    each(chips, lambda off: greet(twin(off)))

    blank = jnp.zeros((2, cols, ch), BF16)

    @pl.when(me == 0)
    def _():
        ext[pl.ds(0, 2)] = blank

    @pl.when(me == n - 1)
    def _():
        ext[pl.ds(rows + 2, 2)] = blank

    pl.semaphore_wait(barrier, chips + 1)

    down = pltpu.make_async_remote_copy(
        src_ref=px.at[pl.ds(rows - 2, 2)], dst_ref=ext.at[pl.ds(0, 2)],
        send_sem=hsend.at[0], recv_sem=hrecv.at[0],
        device_id={"rows": after}, device_id_type=MESH,
    )
    up = pltpu.make_async_remote_copy(
        src_ref=px.at[pl.ds(0, 2)], dst_ref=ext.at[pl.ds(rows + 2, 2)],
        send_sem=hsend.at[1], recv_sem=hrecv.at[1],
        device_id={"rows": before}, device_id_type=MESH,
    )

    @pl.when(me < n - 1)
    def _():
        down.start()

    @pl.when(me > 0)
    def _():
        up.start()

    shape = (2 * ch, hw)
    row, col = index(shape, 0), index(shape, 1)
    mix_sel[...] = selection(col == remainder(row, cw) * 4 + quotient(row, ch // 2), 1.0)
    shape = (rows * cols // 2, rows * cols)
    pair_sel = selection(index(shape, 0) == quotient(index(shape, 1), 2), 0.5)
    shape = (64, rows * cols // 2)
    row, col = index(shape, 0), index(shape, 1)
    part = quotient(row, 16)
    strip = 2 * remainder(part, 2) + quotient(part, 2)
    quad_sel = selection(quotient(col, 2) == strip * lc + remainder(row, lc), 0.5)

    own_pixels.wait()

    @pl.when(me > 0)
    def _():
        down.wait_recv()

    @pl.when(me < n - 1)
    def _():
        up.wait_recv()

    for load in loads[2] + loads[3]:
        load.start()

    pixels = ext[...].reshape((rows + 4) * cols, ch).astype(F32)
    taps = column_taps(pixels, cols)
    summed = jnp.zeros(((rows + 2) * cols, ch), F32)
    for a in range(3):
        loads[0][a].wait()
        summed = summed + dot(taps[a * cols : (a + rows + 2) * cols], w1v[a])
    row = quotient(index(summed.shape, 0), cols)
    outside = ((row == 0) & (me == 0)) | ((row == rows + 1) & (me == n - 1))
    activated = jnp.where(outside, 0.0, silu(summed)).astype(BF16)
    taps = column_taps(activated.astype(F32), cols)
    own = pixels[2 * cols : (rows + 2) * cols]
    for load in loads[1]:
        load.wait()
    chunk = quotient(index((16, ch // 2), 0), lc) == quotient(index((16, ch // 2), 1), cw)

    def make_latent(h):
        lanes = slice(h * ch // 2, (h + 1) * ch // 2)
        conv = dot(taps[: rows * cols], w2v[0, :, lanes])
        for a in range(1, 3):
            conv = conv + dot(taps[a * cols : (a + rows) * cols], w2v[a, :, lanes])
        block_out = (own[:, lanes] + conv).astype(BF16)
        half_res = dot(pair_sel, block_out).astype(BF16)
        quads = dot(quad_sel, half_res)
        pieces = [jnp.where(chunk, quads[16 * q : 16 * q + 16], 0.0).astype(BF16) for q in range(4)]
        return dot(jnp.concatenate(pieces, axis=1), mix_sel[...]).astype(BF16)

    def handover(h):
        return pltpu.make_async_remote_copy(
            src_ref=gathered.at[h, core], dst_ref=gathered.at[h, core],
            send_sem=fsend.at[h], recv_sem=frecv.at[h],
            device_id={"rows": sibling}, device_id_type=MESH,
        )

    def spread(h):
        others = gathered.at[h, core, pl.ds(0, chips - 1)]
        return pltpu.make_async_remote_copy(
            src_ref=others, dst_ref=others, send_sem=gsend.at[h], recv_sem=grecv.at[h],
            device_id={"rows": sibling}, device_id_type=MESH,
        )

    own_latents = []
    for h in range(2):
        own_latents.append(make_latent(h))
        gathered[h, core, pl.ds(chip, 1)] = own_latents[h][None]
        slot = gathered.at[h, core, chip]

        def push_latent(off):
            pltpu.make_async_remote_copy(
                src_ref=slot, dst_ref=slot, send_sem=gsend.at[h], recv_sem=grecv.at[h],
                device_id={"rows": twin(off)}, device_id_type=MESH,
            ).start()

        each(chips, push_latent)

    shape = (gs * 16, gs * 16)
    row, col = index(shape, 0), index(shape, 1)
    place = remainder(quotient(row, lc), gs)
    place = remainder(place, 2) * (gs // 2) + quotient(place, 2)
    wanted = place * 16 + quotient(row, span) * lc + remainder(row, lc)
    sort_sel[...] = selection(col == wanted, 1.0)
    place = quotient(row, 16)
    place = 2 * remainder(place, gs // 2) + quotient(place, gs // 2)
    wanted = remainder(quotient(row, lc), nk) * span + place * lc + remainder(row, lc)
    back_sel[...] = selection(col == wanted, 1.0)
    for load in loads[2]:
        load.wait()
    for h in range(2):
        if chips > 1:
            spread(h).wait_recv()
        handover(h).start()

    width = 2 if oc % 128 == 0 else 1
    groups = [range(first, min(first + width, 9)) for first in range(0, 9, width)]
    terms = [None] * len(groups)
    for h in range(2):
        handover(h).wait_recv()
        for g in range(n // gs):
            block = gathered[h, :, pl.ds(g * gs // 2, gs // 2)].reshape(gs * 16, hw)
            ordered = dot(sort_sel[...], block).astype(BF16)
            for k in range(nk):
                latents[h, pl.ds(g * span, span), pl.ds(k * hw, hw)] = ordered[k * span : (k + 1) * span]
        everywhere = latents[h]
        for at, group in enumerate(groups):
            weights = [wmv[tap // 3, tap % 3, pl.ds(h * nk * hw, nk * hw)] for tap in group]
            weight = weights[0] if len(weights) == 1 else jnp.concatenate(weights, axis=1)
            term = dot(everywhere, weight)
            terms[at] = term if h == 0 else terms[at] + term
    hidden = jnp.zeros((pos, oc), F32)
    for term, group in zip(terms, groups):
        for at, tap in enumerate(group):
            hidden = hidden + latent_tap(term[:, at * oc : (at + 1) * oc], tap, n, lc)
    hidden = silu(hidden).astype(BF16).astype(F32)

    for load in loads[3]:
        load.wait()
    shifted = [latent_tap(hidden, tap, n, lc).astype(BF16) for tap in range(9)]
    if oc % 128 == 0:
        shifted = jnp.concatenate(shifted, axis=1)

    def contribution(start):
        lanes = pl.ds(start, hw)
        if oc % 128 == 0:
            return dot(shifted, wov[:, :, lanes].reshape(9 * oc, hw)).astype(BF16)
        total = jnp.zeros((pos, hw), F32)
        for tap in range(9):
            total = total + dot(shifted[tap], wov[tap // 3, pl.ds(tap % 3 * oc, oc), lanes])
        return total.astype(BF16)

    def swap(h):
        return pltpu.make_async_remote_copy(
            src_ref=outgoing.at[h, 1 - core], dst_ref=swapped.at[h],
            send_sem=xsend.at[h], recv_sem=xrecv.at[h],
            device_id={"rows": sibling}, device_id_type=MESH,
        )

    def scatter(h):
        several = pl.ds(0, chips - 1)
        return pltpu.make_async_remote_copy(
            src_ref=paired.at[h, several], dst_ref=incoming.at[h, several],
            send_sem=ssend.at[h], recv_sem=srecv.at[h],
            device_id={"rows": sibling}, device_id_type=MESH,
        )

    def multiply(h):
        parts = [contribution((h * nk + k) * hw) for k in range(nk)]
        for g in range(n // gs):
            block = jnp.concatenate([part[g * span : (g + 1) * span] for part in parts], axis=0)
            block = dot(back_sel[...], block).astype(BF16).reshape(2, gs // 2, 16, hw)
            outgoing[h, :, pl.ds(g * gs // 2, gs // 2)] = block
        swap(h).start()

    def send_sums(h):
        swap(h).wait_recv()
        paired[h] = (outgoing[h, core].astype(F32) + swapped[h].astype(F32)).astype(BF16)

        def push_sum(off):
            pltpu.make_async_remote_copy(
                src_ref=paired.at[h, chip_at(off)], dst_ref=incoming.at[h, off],
                send_sem=ssend.at[h], recv_sem=srecv.at[h],
                device_id={"rows": twin(off)}, device_id_type=MESH,
            ).start()

        each(chips, push_sum)
        incoming[h, pl.ds(0, 1)] = paired[h, pl.ds(chip, 1)]

    multiply(0)
    multiply(1)
    send_sums(0)
    send_sums(1)

    @pl.when(me < n - 1)
    def _():
        down.wait_send()

    @pl.when(me > 0)
    def _():
        up.wait_send()

    for h in range(2):
        handover(h).wait_send()
        if chips > 1:
            spread(h).wait_send()
    for h in range(2):
        if chips > 1:
            scatter(h).wait_recv()
        total = jnp.sum(incoming[h].astype(F32), axis=0) + own_latents[h].astype(F32)
        for k in range(nk):
            result[0, :, pl.ds((h * nk + k) * hw, hw)] = total[k * lc : (k + 1) * lc].astype(BF16)

    finish = pltpu.make_async_copy(result, out, psem)
    finish.start()
    for h in range(2):
        swap(h).wait_send()
        if chips > 1:
            scatter(h).wait_send()
    finish.wait()


def local(n, pixels, weight_first, weight_second, weight_mix, weight_out):
    rows, cols, ch = pixels.shape
    cl, oc = weight_mix.shape[2:]
    lc = cols // 4
    nk = 16 // lc
    lw = cl // nk
    gs = min(n, 16)
    first = weight_first.reshape(3, 3 * ch, ch)
    second = weight_second.reshape(3, 3 * ch, ch)
    last = weight_out.reshape(3, 3 * oc, cl)
    dma = pltpu.SemaphoreType.DMA
    return pl.pallas_call(
        functools.partial(kernel, n),
        out_shape=jax.ShapeDtypeStruct((rows // 4, lc, cl), BF16),
        in_specs=[pl.BlockSpec(memory_space=pl.ANY)] * 5,
        out_specs=pl.BlockSpec(memory_space=pl.ANY),
        scratch_shapes=[
            pltpu.VMEM((rows + 4, cols, ch), BF16),
            pltpu.VMEM(first.shape, BF16),
            pltpu.VMEM(second.shape, BF16),
            pltpu.VMEM(weight_mix.shape, BF16),
            pltpu.VMEM(last.shape, BF16),
            pltpu.VMEM((2 * ch, lw // 2), BF16),
            pltpu.VMEM((gs * 16, gs * 16), BF16),
            pltpu.VMEM((gs * 16, gs * 16), BF16),
            pltpu.VMEM((2, 2, n // 2, 16, lw // 2), BF16),
            pltpu.VMEM((2, n * lc, cl // 2), BF16),
            pltpu.VMEM((2, 2, n // 2, 16, lw // 2), BF16),
            pltpu.VMEM((2, n // 2, 16, lw // 2), BF16),
            pltpu.VMEM((2, n // 2, 16, lw // 2), BF16),
            pltpu.VMEM((2, n // 2, 16, lw // 2), BF16),
            pltpu.VMEM((rows // 4, lc, cl), BF16),
            dma((4, 3)),
            dma,
            dma((2,)),
            dma((2,)),
            dma((2,)),
            dma((2,)),
            dma((2,)),
            dma((2,)),
            dma((2,)),
            dma((2,)),
            dma((2,)),
            dma((2,)),
        ],
        compiler_params=pltpu.CompilerParams(
            collective_id=0, has_side_effects=True, vmem_limit_bytes=55168 * 1024
        ),
    )(pixels, first, second, weight_mix, last)


def solution(mesh):
    return jax.shard_map(
        functools.partial(local, mesh.shape["rows"]),
        mesh=mesh,
        in_specs=(
            P(("groups", "rows"), None, None),
            P(),
            P(),
            P(None, None, None, "rows"),
            P(None, None, "rows", None),
        ),
        out_specs=P(("groups", "rows"), None, None),
        check_vma=False,
    )
```

```python
import functools

import jax
import jax.numpy as jnp
from jax import lax
from jax.experimental import pallas as pl
from jax.experimental.pallas import tpu as pltpu
from jax.sharding import PartitionSpec as P

MESH = pl.DeviceIdType.MESH
BF16 = jnp.bfloat16
F32 = jnp.float32


def quotient(value, divisor):
    if divisor & (divisor - 1) == 0:
        return lax.shift_right_logical(value, divisor.bit_length() - 1)
    return value // divisor


def remainder(value, divisor):
    if divisor & (divisor - 1) == 0:
        return value & (divisor - 1)
    return value % divisor


def index(shape, dim):
    return lax.broadcasted_iota(jnp.int32, shape, dim)


def selection(mask, entry):
    return jnp.where(mask, entry, 0.0).astype(BF16)


def dot(left, right):
    return jnp.dot(left, right, preferred_element_type=F32)


def silu(value):
    return value / (1.0 + jnp.exp(-value))


def column_taps(value, cols):
    length = value.shape[0]
    col = remainder(index(value.shape, 0), cols)
    left = jnp.where(col == 0, 0.0, pltpu.roll(value, 1, 0))
    right = jnp.where(col == cols - 1, 0.0, pltpu.roll(value, length - 1, 0))
    return jnp.concatenate([left.astype(BF16), value.astype(BF16), right.astype(BF16)], axis=1)


def latent_tap(value, tap, rows, cols):
    row_step, col_step = tap // 3 - 1, tap % 3 - 1
    step = row_step * cols + col_step
    if step == 0:
        return value
    length = rows * cols
    place = index(value.shape, 0)
    row, col = quotient(place, cols) + row_step, remainder(place, cols) + col_step
    inside = (row >= 0) & (row < rows) & (col >= 0) & (col < cols)
    return jnp.where(inside, pltpu.roll(value, (-step) % length, 0), 0.0)


def each(count, body):
    if count <= 16:
        for off in range(1, count):
            body(off)
        return

    def step(off, carry):
        body(off)
        return carry

    lax.fori_loop(1, count, step, 0)


def kernel(
    n, px, w1, w2, wm, wo, out,
    ext, w1v, w2v, wmv, wov, mix_sel, sort_sel, back_sel, gathered, latents, outgoing, swapped, paired, incoming, result,
    wsem, psem, hsend, hrecv, gsend, grecv, fsend, frecv, xsend, xrecv, ssend, srecv,
):
    me = lax.axis_index("rows")
    core, chip, chips = me & 1, lax.shift_right_logical(me, 1), n // 2
    sibling = me + 1 - 2 * core
    even = chips & (chips - 1) == 0
    rows, cols, ch = px.shape
    oc = wmv.shape[-1]
    lc = cols // 4
    nk = 16 // lc
    lw = 4 * ch // nk
    cw = ch // (2 * nk)
    gs = min(n, 16)
    span = gs * lc
    pos = n * lc
    hw = lw // 2

    def chip_at(off):
        return chip ^ off if even else lax.rem(chip + off, chips)

    def twin(off):
        return 2 * chip_at(off) + core

    own_pixels = pltpu.make_async_copy(px, ext.at[pl.ds(2, rows)], psem)
    own_pixels.start()
    loads = []
    for which, (src, dst) in enumerate(((w1, w1v), (w2, w2v), (wm, wmv), (wo, wov))):
        loads.append([pltpu.make_async_copy(src.at[a], dst.at[a], wsem.at[which, a]) for a in range(3)])
    for load in loads[0] + loads[1]:
        load.start()

    barrier = pltpu.get_barrier_semaphore()

    def greet(peer):
        pl.semaphore_signal(barrier, inc=1, device_id={"rows": peer}, device_id_type=MESH)

    before, after = jnp.where(me == 0, n - 1, me - 1), jnp.where(me == n - 1, 0, me + 1)
    greet(jnp.where(core == 0, before, after))
    greet(sibling)
    each(chips, lambda off: greet(twin(off)))

    blank = jnp.zeros((2, cols, ch), BF16)

    @pl.when(me == 0)
    def _():
        ext[pl.ds(0, 2)] = blank

    @pl.when(me == n - 1)
    def _():
        ext[pl.ds(rows + 2, 2)] = blank

    pl.semaphore_wait(barrier, chips + 1)

    down = pltpu.make_async_remote_copy(
        src_ref=px.at[pl.ds(rows - 2, 2)], dst_ref=ext.at[pl.ds(0, 2)],
        send_sem=hsend.at[0], recv_sem=hrecv.at[0],
        device_id={"rows": after}, device_id_type=MESH,
    )
    up = pltpu.make_async_remote_copy(
        src_ref=px.at[pl.ds(0, 2)], dst_ref=ext.at[pl.ds(rows + 2, 2)],
        send_sem=hsend.at[1], recv_sem=hrecv.at[1],
        device_id={"rows": before}, device_id_type=MESH,
    )

    @pl.when(me < n - 1)
    def _():
        down.start()

    @pl.when(me > 0)
    def _():
        up.start()

    shape = (2 * ch, hw)
    row, col = index(shape, 0), index(shape, 1)
    mix_sel[...] = selection(col == remainder(row, cw) * 4 + quotient(row, ch // 2), 1.0)
    shape = (rows * cols // 2, rows * cols)
    pair_sel = selection(index(shape, 0) == quotient(index(shape, 1), 2), 0.5)
    shape = (64, rows * cols // 2)
    row, col = index(shape, 0), index(shape, 1)
    part = quotient(row, 16)
    strip = 2 * remainder(part, 2) + quotient(part, 2)
    quad_sel = selection(quotient(col, 2) == strip * lc + remainder(row, lc), 0.5)

    own_pixels.wait()

    @pl.when(me > 0)
    def _():
        down.wait_recv()

    @pl.when(me < n - 1)
    def _():
        up.wait_recv()

    for load in loads[2] + loads[3]:
        load.start()

    pixels = ext[...].reshape((rows + 4) * cols, ch).astype(F32)
    taps = column_taps(pixels, cols)
    summed = jnp.zeros(((rows + 2) * cols, ch), F32)
    for a in range(3):
        loads[0][a].wait()
        summed = summed + dot(taps[a * cols : (a + rows + 2) * cols], w1v[a])
    row = quotient(index(summed.shape, 0), cols)
    outside = ((row == 0) & (me == 0)) | ((row == rows + 1) & (me == n - 1))
    activated = jnp.where(outside, 0.0, silu(summed)).astype(BF16)
    taps = column_taps(activated.astype(F32), cols)
    own = pixels[2 * cols : (rows + 2) * cols]
    for load in loads[1]:
        load.wait()
    chunk = quotient(index((16, ch // 2), 0), lc) == quotient(index((16, ch // 2), 1), cw)

    def make_latent(h):
        lanes = slice(h * ch // 2, (h + 1) * ch // 2)
        conv = dot(taps[: rows * cols], w2v[0, :, lanes])
        for a in range(1, 3):
            conv = conv + dot(taps[a * cols : (a + rows) * cols], w2v[a, :, lanes])
        block_out = (own[:, lanes] + conv).astype(BF16)
        half_res = dot(pair_sel, block_out).astype(BF16)
        quads = dot(quad_sel, half_res)
        pieces = [jnp.where(chunk, quads[16 * q : 16 * q + 16], 0.0).astype(BF16) for q in range(4)]
        return dot(jnp.concatenate(pieces, axis=1), mix_sel[...]).astype(BF16)

    def handover(h):
        return pltpu.make_async_remote_copy(
            src_ref=gathered.at[h, core], dst_ref=gathered.at[h, core],
            send_sem=fsend.at[h], recv_sem=frecv.at[h],
            device_id={"rows": sibling}, device_id_type=MESH,
        )

    def spread(h):
        others = gathered.at[h, core, pl.ds(0, chips - 1)]
        return pltpu.make_async_remote_copy(
            src_ref=others, dst_ref=others, send_sem=gsend.at[h], recv_sem=grecv.at[h],
            device_id={"rows": sibling}, device_id_type=MESH,
        )

    own_latents = []
    for h in range(2):
        own_latents.append(make_latent(h))
        gathered[h, core, pl.ds(chip, 1)] = own_latents[h][None]
        slot = gathered.at[h, core, chip]

        def push_latent(off):
            pltpu.make_async_remote_copy(
                src_ref=slot, dst_ref=slot, send_sem=gsend.at[h], recv_sem=grecv.at[h],
                device_id={"rows": twin(off)}, device_id_type=MESH,
            ).start()

        each(chips, push_latent)

    shape = (gs * 16, gs * 16)
    row, col = index(shape, 0), index(shape, 1)
    place = remainder(quotient(row, lc), gs)
    place = remainder(place, 2) * (gs // 2) + quotient(place, 2)
    wanted = place * 16 + quotient(row, span) * lc + remainder(row, lc)
    sort_sel[...] = selection(col == wanted, 1.0)
    place = quotient(row, 16)
    place = 2 * remainder(place, gs // 2) + quotient(place, gs // 2)
    wanted = remainder(quotient(row, lc), nk) * span + place * lc + remainder(row, lc)
    back_sel[...] = selection(col == wanted, 1.0)
    for load in loads[2]:
        load.wait()
    for h in range(2):
        if chips > 1:
            spread(h).wait_recv()
        handover(h).start()

    width = 2 if oc % 128 == 0 else 1
    groups = [range(first, min(first + width, 9)) for first in range(0, 9, width)]
    terms = [None] * len(groups)
    for h in range(2):
        handover(h).wait_recv()
        for g in range(n // gs):
            block = gathered[h, :, pl.ds(g * gs // 2, gs // 2)].reshape(gs * 16, hw)
            ordered = dot(sort_sel[...], block).astype(BF16)
            for k in range(nk):
                latents[h, pl.ds(g * span, span), pl.ds(k * hw, hw)] = ordered[k * span : (k + 1) * span]
        everywhere = latents[h]
        for at, group in enumerate(groups):
            weights = [wmv[tap // 3, tap % 3, pl.ds(h * nk * hw, nk * hw)] for tap in group]
            weight = weights[0] if len(weights) == 1 else jnp.concatenate(weights, axis=1)
            term = dot(everywhere, weight)
            terms[at] = term if h == 0 else terms[at] + term
    hidden = jnp.zeros((pos, oc), F32)
    for term, group in zip(terms, groups):
        for at, tap in enumerate(group):
            hidden = hidden + latent_tap(term[:, at * oc : (at + 1) * oc], tap, n, lc)
    hidden = silu(hidden).astype(BF16).astype(F32)

    for load in loads[3]:
        load.wait()
    shifted = [latent_tap(hidden, tap, n, lc).astype(BF16) for tap in range(9)]
    if oc % 128 == 0:
        shifted = jnp.concatenate(shifted, axis=1)

    def contribution(start):
        lanes = pl.ds(start, hw)
        if oc % 128 == 0:
            return dot(shifted, wov[:, :, lanes].reshape(9 * oc, hw)).astype(BF16)
        total = jnp.zeros((pos, hw), F32)
        for tap in range(9):
            total = total + dot(shifted[tap], wov[tap // 3, pl.ds(tap % 3 * oc, oc), lanes])
        return total.astype(BF16)

    def swap(h):
        return pltpu.make_async_remote_copy(
            src_ref=outgoing.at[h, 1 - core], dst_ref=swapped.at[h],
            send_sem=xsend.at[h], recv_sem=xrecv.at[h],
            device_id={"rows": sibling}, device_id_type=MESH,
        )

    def scatter(h):
        several = pl.ds(0, chips - 1)
        return pltpu.make_async_remote_copy(
            src_ref=paired.at[h, several], dst_ref=incoming.at[h, several],
            send_sem=ssend.at[h], recv_sem=srecv.at[h],
            device_id={"rows": sibling}, device_id_type=MESH,
        )

    def multiply(h):
        parts = []
        for k in range(nk):
            if h == 1 and k == nk - 1:
                send_sums(0)
            parts.append(contribution((h * nk + k) * hw))
        for g in range(n // gs):
            block = jnp.concatenate([part[g * span : (g + 1) * span] for part in parts], axis=0)
            block = dot(back_sel[...], block).astype(BF16).reshape(2, gs // 2, 16, hw)
            outgoing[h, :, pl.ds(g * gs // 2, gs // 2)] = block
        swap(h).start()

    def send_sums(h):
        swap(h).wait_recv()
        paired[h] = (outgoing[h, core].astype(F32) + swapped[h].astype(F32)).astype(BF16)

        def push_sum(off):
            pltpu.make_async_remote_copy(
                src_ref=paired.at[h, chip_at(off)], dst_ref=incoming.at[h, off],
                send_sem=ssend.at[h], recv_sem=srecv.at[h],
                device_id={"rows": twin(off)}, device_id_type=MESH,
            ).start()

        each(chips, push_sum)
        incoming[h, pl.ds(0, 1)] = paired[h, pl.ds(chip, 1)]

    multiply(0)
    multiply(1)
    send_sums(1)

    @pl.when(me < n - 1)
    def _():
        down.wait_send()

    @pl.when(me > 0)
    def _():
        up.wait_send()

    for h in range(2):
        handover(h).wait_send()
        if chips > 1:
            spread(h).wait_send()
    for h in range(2):
        if chips > 1:
            scatter(h).wait_recv()
        total = jnp.sum(incoming[h].astype(F32), axis=0) + own_latents[h].astype(F32)
        for k in range(nk):
            result[0, :, pl.ds((h * nk + k) * hw, hw)] = total[k * lc : (k + 1) * lc].astype(BF16)

    finish = pltpu.make_async_copy(result, out, psem)
    finish.start()
    for h in range(2):
        swap(h).wait_send()
        if chips > 1:
            scatter(h).wait_send()
    finish.wait()


def local(n, pixels, weight_first, weight_second, weight_mix, weight_out):
    rows, cols, ch = pixels.shape
    cl, oc = weight_mix.shape[2:]
    lc = cols // 4
    nk = 16 // lc
    lw = cl // nk
    gs = min(n, 16)
    first = weight_first.reshape(3, 3 * ch, ch)
    second = weight_second.reshape(3, 3 * ch, ch)
    last = weight_out.reshape(3, 3 * oc, cl)
    dma = pltpu.SemaphoreType.DMA
    return pl.pallas_call(
        functools.partial(kernel, n),
        out_shape=jax.ShapeDtypeStruct((rows // 4, lc, cl), BF16),
        in_specs=[pl.BlockSpec(memory_space=pl.ANY)] * 5,
        out_specs=pl.BlockSpec(memory_space=pl.ANY),
        scratch_shapes=[
            pltpu.VMEM((rows + 4, cols, ch), BF16),
            pltpu.VMEM(first.shape, BF16),
            pltpu.VMEM(second.shape, BF16),
            pltpu.VMEM(weight_mix.shape, BF16),
            pltpu.VMEM(last.shape, BF16),
            pltpu.VMEM((2 * ch, lw // 2), BF16),
            pltpu.VMEM((gs * 16, gs * 16), BF16),
            pltpu.VMEM((gs * 16, gs * 16), BF16),
            pltpu.VMEM((2, 2, n // 2, 16, lw // 2), BF16),
            pltpu.VMEM((2, n * lc, cl // 2), BF16),
            pltpu.VMEM((2, 2, n // 2, 16, lw // 2), BF16),
            pltpu.VMEM((2, n // 2, 16, lw // 2), BF16),
            pltpu.VMEM((2, n // 2, 16, lw // 2), BF16),
            pltpu.VMEM((2, n // 2, 16, lw // 2), BF16),
            pltpu.VMEM((rows // 4, lc, cl), BF16),
            dma((4, 3)),
            dma,
            dma((2,)),
            dma((2,)),
            dma((2,)),
            dma((2,)),
            dma((2,)),
            dma((2,)),
            dma((2,)),
            dma((2,)),
            dma((2,)),
            dma((2,)),
        ],
        compiler_params=pltpu.CompilerParams(
            collective_id=0, has_side_effects=True, vmem_limit_bytes=55168 * 1024
        ),
    )(pixels, first, second, weight_mix, last)


def solution(mesh):
    return jax.shard_map(
        functools.partial(local, mesh.shape["rows"]),
        mesh=mesh,
        in_specs=(
            P(("groups", "rows"), None, None),
            P(),
            P(),
            P(None, None, None, "rows"),
            P(None, None, "rows", None),
        ),
        out_specs=P(("groups", "rows"), None, None),
        check_vma=False,
    )
```
